512 devices in a mesh: row: 32 (over z, core), col: 16 (over x, y).
Axes of the slice: x: 4, y: 4, z: 16, core: 2. Of those that a mesh axis runs over, the one named last changes fastest.
Arguments:
- tokens: bfloat16 [262144, 1024], P(('row', 'col')), may hold values from -64 to 64, as said below
- merge_map: int32 [262144], P(('row', 'col')), may hold values from 0 to 511, as said below
- block_owner: int32 [512, 8], P(('row', 'col')), may hold values from -1 to 63, as said below
- neighbours: int32 [1024, 16], P(('row', 'col')), may hold values from 0 to 31, as said below
- w_query: bfloat16 [1024, 512], replicated, may hold values from -0.1875 to 0.1875
- w_key: bfloat16 [1024, 512], replicated, may hold values from -0.1875 to 0.1875
- w_value: bfloat16 [1024, 512], replicated, may hold values from -0.1875 to 0.1875
Outputs:
- attended: bfloat16 [262144, 512], P(('row', 'col'))
The draws below stay inside these ranges and needn't reach their ends.
Inputs may be any that keep to these rules, and one draw needn't show every extreme that they name: `merge_map`: within a tile, the slots of its live blocks (those whose block_owner is not -1) are each used by one or more tokens, and no other slot is used. `block_owner`: A tile's live blocks are its first ones, 1 to 8 of them, 8 in some tile of every column index; a code o names owned block o % 2 of the device with row index o // 2 and the tile's column index; within one column index every code is named exactly once; one tile names each row index at most once. `neighbours`: the entries of a row are distinct, and the first is the block's own candidate number. `tokens`: finite bfloat16 values.
All inputs are finite; a program needn't handle non-finite values.
Results may differ from the reference program's by a relative error of at most 0.019.
The reference program's roundings to bfloat16 on the way count: a program that leaves them out, or rounds other values in their place, can miss the bound.
Values may be sent and summed in bfloat16 or wider, within the bound.
A program may use at most 64 MiB of HBM per device.

```python
import math
import jax
import jax.numpy as jnp
from jax import lax

D = 1024
HEADS = 8
HD = 64
BLK = 64
OWN = 2
SLOTS_BLK = 8
TOK_DEV = 512
TOKENS = 262144
BLOCKS = 1024
NB = 16
N_ROW = 32
N_COL = 16


def live_blocks(key):
    pattern = jnp.array([8, 2, 1, 1, 1, 1, 1, 1], jnp.int32)
    row_kind = pattern[jnp.arange(N_ROW, dtype=jnp.int32) % 8]
    col_keys = jax.random.split(jax.random.fold_in(key, 11), N_COL)

    def column(col_key):
        shuffled = jax.random.permutation(col_key, N_ROW)
        return row_kind[shuffled]
    per_col = jax.vmap(column)(col_keys)
    return per_col.T.reshape(-1)


def draw_block_owner(key, part):
    live_count = live_blocks(key).reshape(N_ROW, N_COL)
    row_start = jnp.cumsum(live_count, axis=0) - live_count
    block_ids = jnp.arange(SLOTS_BLK, dtype=jnp.int32)
    ranked = row_start[:, :, None] + block_ids[None, None, :]
    dest_code = ranked % N_ROW * OWN + ranked // N_ROW
    result = jnp.where(block_ids[None, None, :] < live_count[:, :, None], dest_code, -1)
    return result.reshape(N_ROW * N_COL, SLOTS_BLK).astype(jnp.int32)


def draw_merge_map(key, part):
    live_count = live_blocks(key)
    used_slots = live_count * BLK
    tile_keys = jax.random.split(jax.random.fold_in(key, 23), N_ROW * N_COL)

    def tile(tile_key, used):
        first_key, second_key = jax.random.split(tile_key)
        shuffled = jax.random.permutation(first_key, TOK_DEV)
        position = jnp.argsort(shuffled).astype(jnp.int32)
        spare_slot = jax.random.randint(second_key, (TOK_DEV,), 0, used)
        return jnp.where(position < used, position, spare_slot)
    return jax.vmap(tile)(tile_keys, used_slots).reshape(-1).astype(jnp.int32)


def draw_neighbours(key, part):
    cand_total = N_COL * OWN
    block_keys = jax.random.split(jax.random.fold_in(key, 37), BLOCKS)
    block_ids = jnp.arange(BLOCKS, dtype=jnp.int32)
    self_ids = block_ids // OWN % N_COL * OWN + block_ids % OWN

    def listing(block_key, self_id):
        shuffled = jax.random.permutation(block_key, cand_total)
        rank_key = jnp.where(shuffled == self_id, -1, jnp.arange(cand_total, dtype=jnp.int32))
        return shuffled[jnp.argsort(rank_key)][:NB]
    return jax.vmap(listing)(block_keys, self_ids).astype(jnp.int32)


def draw_tokens(key, part):
    normals = jax.random.truncated_normal(key, -4.0, 4.0, (TOKENS, D), jnp.float32)
    return normals.astype(jnp.bfloat16)


def normal_values(stream_key, extent, deviation, limit, kind=jnp.bfloat16):
    return jnp.clip(deviation * jax.random.normal(stream_key, extent, jnp.float32), -limit, limit).astype(kind)


def setup_inputs(seed: int = 0) -> dict:
    arg_keys = jax.random.split(jax.random.key(seed), 8)
    tokens = draw_tokens(jax.random.fold_in(arg_keys[7], 71), 0)
    merge_map = draw_merge_map(jax.random.fold_in(arg_keys[7], 71), 0)
    block_owner = draw_block_owner(jax.random.fold_in(arg_keys[7], 71), 0)
    neighbours = draw_neighbours(jax.random.fold_in(arg_keys[7], 71), 0)
    w_query = normal_values(arg_keys[4], (D, HEADS * HD), D ** -0.5, 0.1875)
    w_key = normal_values(arg_keys[5], (D, HEADS * HD), D ** -0.5, 0.1875)
    w_value = normal_values(arg_keys[6], (D, HEADS * HD), D ** -0.5, 0.1875)
    return dict(tokens=tokens, merge_map=merge_map, block_owner=block_owner, neighbours=neighbours, w_query=w_query, w_key=w_key, w_value=w_value)


def reference(tokens, merge_map, block_owner, neighbours, w_query, w_key, w_value):
    tile_count = N_ROW * N_COL
    slot_total = SLOTS_BLK * BLK
    head_width = HEADS * HD
    cand_total = N_COL * OWN
    tok_tiles = tokens.reshape(tile_count, TOK_DEV, D)
    map_tiles = merge_map.reshape(tile_count, TOK_DEV)

    def merge_tile(pair):
        tile_rows, mapping = pair
        onehot = (jnp.arange(slot_total, dtype=jnp.int32)[:, None] == mapping[None, :]).astype(jnp.float32)
        slot_sums = jnp.dot(onehot, tile_rows.astype(jnp.float32), precision=lax.Precision.HIGHEST)
        slot_count = lax.optimization_barrier(jnp.sum(onehot, axis=1))
        return (slot_sums / jnp.maximum(slot_count, 1.0)[:, None]).astype(jnp.bfloat16)
    merged = lax.map(merge_tile, (tok_tiles, map_tiles))
    blocks = merged.reshape(tile_count * SLOTS_BLK, BLK, D)
    tile_ids = jnp.arange(tile_count, dtype=jnp.int32)[:, None]
    target = (block_owner // OWN * N_COL + tile_ids % N_COL) * OWN + block_owner % OWN
    target = jnp.where(block_owner >= 0, target, BLOCKS).reshape(-1).astype(jnp.int32)
    owned_blocks = jnp.zeros((BLOCKS, BLK, D), jnp.bfloat16).at[target].set(blocks, mode='drop')
    score_scale = 1.0 / math.sqrt(HD)

    def attend_row(pair):
        row_blocks, cand_lists = pair
        row_tokens = row_blocks.reshape(-1, D)
        query_rows = jnp.dot(row_tokens, w_query, preferred_element_type=jnp.float32).astype(jnp.bfloat16)
        key_rows = jnp.dot(row_tokens, w_key, preferred_element_type=jnp.float32).astype(jnp.bfloat16)
        value_rows = jnp.dot(row_tokens, w_value, preferred_element_type=jnp.float32).astype(jnp.bfloat16)
        query_heads = query_rows.reshape(-1, HEADS, HD).astype(jnp.float32)
        key_heads = key_rows.reshape(-1, HEADS, HD).astype(jnp.float32)
        value_heads = value_rows.reshape(-1, HEADS, HD).astype(jnp.float32)
        scores = jnp.einsum('qhd,khd->hqk', query_heads, key_heads) * score_scale
        allowed = jnp.any(cand_lists[:, :, None] == jnp.arange(cand_total, dtype=jnp.int32)[None, None, :], axis=1)
        visible = jnp.repeat(jnp.repeat(allowed, BLK, axis=0), BLK, axis=1)[None]
        scores = jnp.where(visible, scores, -1e+30)
        row_max = lax.optimization_barrier(jnp.max(scores, axis=-1, keepdims=True))
        probs = jnp.where(visible, jnp.exp(scores - row_max), 0.0)
        weight_total = lax.optimization_barrier(jnp.sum(probs, axis=-1, keepdims=True))
        weights = probs.astype(jnp.bfloat16).astype(jnp.float32)
        head_out = jnp.einsum('hqk,khd->hqd', weights, value_heads) / weight_total
        return head_out.transpose(1, 0, 2).reshape(-1, head_width).astype(jnp.bfloat16)
    attended_rows = lax.map(attend_row, (owned_blocks.reshape(N_ROW, cand_total, BLK, D), neighbours.reshape(N_ROW, cand_total, NB)))
    attended_rows = attended_rows.reshape(-1, head_width)
    block_of = map_tiles // BLK
    dest_code = jnp.take_along_axis(block_owner, block_of, axis=1)
    token_index = ((dest_code // OWN * N_COL + tile_ids % N_COL) * OWN + dest_code % OWN) * BLK + map_tiles % BLK
    return attended_rows[token_index.reshape(-1).astype(jnp.int32)]
```

```python
import functools
import math

import jax
import jax.numpy as jnp
from jax import lax
from jax.experimental import pallas as pl
from jax.experimental.pallas import tpu as pltpu
from jax.sharding import PartitionSpec as P

HD = 64
BLK = 64
OWN = 2
SLOTS_BLK = 8
STEPS = 16
DELAY = 2
MESH = pl.DeviceIdType.MESH


def on_device(tokens, merge_map, block_owner, neighbours, w_query, w_key, w_value):
    row_count = lax.axis_size("row")
    col_count = lax.axis_size("col")
    slot_total = SLOTS_BLK * BLK
    width = tokens.shape[1]
    head_width = w_query.shape[1]
    heads = head_width // HD
    cand_total = col_count * OWN
    query_count = OWN * BLK
    score_scale = 1.0 / math.sqrt(HD)
    slot_ids = lax.broadcasted_iota(jnp.int32, (slot_total, tokens.shape[0]), 0)
    onehot = (slot_ids == merge_map[None, :]).astype(jnp.bfloat16)
    slot_sums = jnp.dot(onehot, tokens, preferred_element_type=jnp.float32)
    slot_count = jnp.sum(onehot.astype(jnp.float32), axis=1)
    merged = (slot_sums / jnp.maximum(slot_count, 1.0)[:, None]).astype(jnp.bfloat16)
    dest_code = block_owner[0]
    dest_row = dest_code // OWN
    merged_blocks = merged.reshape(SLOTS_BLK, BLK * width)
    peer_ids = lax.broadcasted_iota(jnp.int32, (row_count, SLOTS_BLK), 0)
    select = (peer_ids == dest_row[None, :]) & (dest_code[None, :] >= 0)
    outgoing = jnp.dot(
        select.astype(jnp.bfloat16), merged_blocks, preferred_element_type=jnp.float32
    )
    outgoing = outgoing.astype(jnp.bfloat16).reshape(row_count, BLK, width)
    slot_tag = jnp.sum(jnp.where(select, dest_code[None, :] % OWN + 1, 0), axis=1) - 1
    arrived = lax.all_to_all(outgoing, "row", split_axis=0, concat_axis=0, tiled=True)
    arrived_tag = lax.all_to_all(slot_tag, "row", split_axis=0, concat_axis=0, tiled=True)
    own_ids = lax.broadcasted_iota(jnp.int32, (OWN, row_count), 0)
    place_map = (own_ids == arrived_tag[None, :]).astype(jnp.bfloat16)
    owned_tokens = jnp.dot(
        place_map, arrived.reshape(row_count, BLK * width), preferred_element_type=jnp.float32
    )
    owned_tokens = owned_tokens.astype(jnp.bfloat16).reshape(query_count, width)
    query_rows = jnp.dot(owned_tokens, w_query, preferred_element_type=jnp.float32).astype(
        jnp.bfloat16
    )
    query_heads = query_rows.reshape(query_count, heads, HD)
    cand_ids = lax.broadcasted_iota(jnp.int32, (1, 1, cand_total), 2)
    allowed = jnp.any(neighbours[:, :, None] == cand_ids, axis=1)
    token_piece = lax.all_gather(owned_tokens, "col", axis=0, tiled=True)
    key_rows = jnp.dot(token_piece, w_key, preferred_element_type=jnp.float32).astype(jnp.bfloat16)
    value_rows = jnp.dot(token_piece, w_value, preferred_element_type=jnp.float32).astype(
        jnp.bfloat16
    )
    key_count = key_rows.shape[0]
    key_heads = key_rows.reshape(key_count, heads, HD)
    value_heads = value_rows.reshape(key_count, heads, HD)
    scores = (
        jnp.einsum("qhd,khd->hqk", query_heads, key_heads, preferred_element_type=jnp.float32)
        * score_scale
    )
    visible = jnp.repeat(jnp.repeat(allowed, BLK, axis=0), BLK, axis=1)[None]
    scores = jnp.where(visible, scores, -1e30)
    new_max = jnp.max(scores, axis=-1)
    probs = jnp.where(visible, jnp.exp(scores - new_max[..., None]), 0.0)
    new_sum = jnp.sum(probs, axis=-1)
    product = jnp.einsum(
        "hqk,khd->hqd", probs.astype(jnp.bfloat16), value_heads, preferred_element_type=jnp.float32
    )
    head_out = (
        (product / new_sum[..., None])
        .transpose(1, 0, 2)
        .reshape(query_count, head_width)
        .astype(jnp.bfloat16)
    )
    reply_map = (
        lax.broadcasted_iota(jnp.int32, (row_count, OWN), 1) == arrived_tag[:, None]
    ).astype(jnp.bfloat16)
    replies = jnp.dot(
        reply_map, head_out.reshape(OWN, BLK * head_width), preferred_element_type=jnp.float32
    )
    replies = replies.astype(jnp.bfloat16).reshape(row_count, BLK, head_width)
    returned = lax.all_to_all(replies, "row", split_axis=0, concat_axis=0, tiled=True)
    returned_rows = returned.reshape(row_count * BLK, head_width)
    token_block = merge_map // BLK
    block_ids = lax.broadcasted_iota(jnp.int32, (1, SLOTS_BLK), 1)
    token_dest = jnp.sum(jnp.where(token_block[:, None] == block_ids, dest_row[None, :], 0), axis=1)
    token_index = token_dest * BLK + merge_map % BLK
    return jnp.take(returned_rows, token_index, axis=0)


def plan_routes(rx_codes, tbl_v, nz, z, steps):
    shape = (max(nz, 8), 128)
    lane = lax.broadcasted_iota(jnp.int32, shape, 1)
    chip = lax.broadcasted_iota(jnp.int32, shape, 0)
    place = jnp.sum(rx_codes, axis=0)
    place = jnp.sum(place, axis=0, keepdims=True)
    place = jnp.broadcast_to(place, shape)
    valid = place > 0
    place = place - 1
    pos = jnp.where(valid, place >> 4, 0)
    loc = jnp.where(valid, place & 15, 0)
    fwd = ((lane >> 2) - pos) & (nz - 1)
    half = nz // 2
    right = (fwd < half) | ((fwd == half) & ((lane & 1) == 0))
    rem = jnp.where(valid, jnp.where(right, fwd, nz - fwd), 0)
    right_i = right.astype(jnp.int32)
    mine = chip == z
    back = jnp.full(shape, 2 * steps, jnp.int32)

    def step(t, state):
        pos, rem, ready, loc, send, back = state
        open_ = (rem > 0) & (ready <= t) & (pos == chip)
        key = rem * 128 + lane + 1
        for d in range(2):
            here = open_ & (right_i == 1 - d)
            keyed = jnp.where(here, key, 0)
            best = jnp.max(keyed, axis=1, keepdims=True)
            pick = jnp.where(here & (keyed == best), 1, 0)
            moved = jnp.broadcast_to(jnp.max(pick, axis=0, keepdims=True), shape) > 0
            own = jnp.sum(jnp.where(mine, pick * (loc + 1), 0), axis=1, keepdims=True)
            own = jnp.broadcast_to(jnp.sum(own, axis=0, keepdims=True), shape)
            slot = 2 * t + d
            send = jnp.where(lane == slot, jnp.maximum(own - 1, 0), send)
            back = jnp.where(lane == own - 1, slot, back)
            pos = jnp.where(moved, (pos + (1 - 2 * d)) & (nz - 1), pos)
            rem = jnp.where(moved, rem - 1, rem)
            ready = jnp.where(moved, t + DELAY, ready)
            loc = jnp.where(moved, 16 + slot, loc)
        return pos, rem, ready, loc, send, back

    zero = jnp.zeros(shape, jnp.int32)
    pos, rem, ready, loc, send, back = lax.fori_loop(
        0, steps, step, (pos, rem, zero, loc, zero, back)
    )
    final = zero
    for i in range(2 * OWN):
        at = jnp.sum(jnp.where(lane == 2 * OWN * z + i, loc, 0), axis=1, keepdims=True)
        at = jnp.broadcast_to(at, shape)
        back = jnp.where(lane == at, 2 * steps + i, back)
        final = jnp.where(lane == i, at, final)
    row8 = lax.broadcasted_iota(jnp.int32, (8, 128), 0)
    table = jnp.where(row8 == 0, send[:8], jnp.where(row8 == 1, back[:8], final[:8]))
    tbl_v[...] = table
    return jnp.broadcast_to(jnp.max(rem, axis=1, keepdims=True), shape)[:8]


def kernel(
    dims,
    tokens_hbm, map_ref, owner_ref, nb_ref, wq_hbm, wk_hbm, wv_hbm,
    out_ref, flag_ref,
    tok, wts, onehot, onehot_t,
    codes_tx, codes_rx, tbl_v, tbl_s,
    local, sib_tx, sib_rx, stage, recv, fin_tx, fin_rx, owned,
    msg_tx, msg_rx, pairs, nb_tx, nb_rx, nb_s,
    att_tx, att_rx, home, ret_stage, ret_recv, ret_tx, ret_rx,
    load_sem, codes_ssem, codes_rsem, pair_ssem, pair_rsem, hop_ssem, hop_rsem,
    msg_ssem, msg_rsem, nb_ssem, nb_rsem, att_ssem, att_rsem, ret_ssem, ret_rsem,
):
    nrow, ncol, heads, width, steps = dims
    nz = nrow // 2
    half = width // 2
    hh = heads // 2
    hw = hh * HD
    half_col = ncol // 2
    slots = SLOTS_BLK * BLK
    row = lax.axis_index("row")
    col = lax.axis_index("col")
    z = row // 2
    core = lax.rem(row, 2)
    sib = row + 1 - 2 * core
    barrier = pltpu.get_barrier_semaphore()

    loads = [pltpu.make_async_copy(tokens_hbm, tok, load_sem.at[0])]
    for i, w in enumerate((wq_hbm, wk_hbm, wv_hbm)):
        loads.append(pltpu.make_async_copy(w, wts.at[i], load_sem.at[i + 1]))
    for load in loads:
        load.start()

    @pl.loop(1, nrow)
    def _(i):
        pl.semaphore_signal(
            barrier, inc=1, device_id=(lax.rem(row + i, nrow), col), device_id_type=MESH
        )

    @pl.loop(1, ncol)
    def _(i):
        other = lax.rem(col + i, ncol)
        pl.semaphore_signal(barrier, inc=1, device_id=(row, other), device_id_type=MESH)
        pl.semaphore_signal(barrier, inc=1, device_id=(sib, other), device_id_type=MESH)

    lane8 = lax.broadcasted_iota(jnp.int32, (8, 128), 1)
    row8 = lax.broadcasted_iota(jnp.int32, (8, 128), 0)
    codes = jnp.zeros((8, 128), jnp.int32)
    for b in range(SLOTS_BLK):
        codes = jnp.where((lane8 == owner_ref[0, b]) & (row8 == 0), row * 8 + b + 1, codes)
    codes_tx[...] = codes
    codes_rx[row] = codes

    slot_ids = lax.broadcasted_iota(jnp.int32, (slots, map_ref.shape[1]), 0)
    hot = jnp.where(slot_ids == map_ref[...], 1.0, 0.0).astype(jnp.bfloat16)
    onehot[...] = hot
    count = jnp.dot(
        hot, jnp.ones((map_ref.shape[1], 128), jnp.bfloat16), preferred_element_type=jnp.float32
    )
    share = 1.0 / jnp.maximum(count, 1.0)

    def merge(which, dst, base):
        sums = jnp.dot(
            onehot[...],
            tok[:, pl.ds(pl.multiple_of(which * half, 128), half)],
            preferred_element_type=jnp.float32,
        )
        for i in range(half // 128):
            cols = slice(i * 128, (i + 1) * 128)
            part = (sums[:, cols] * share).astype(jnp.bfloat16)
            dst[pl.ds(base, SLOTS_BLK), :, cols] = part.reshape(SLOTS_BLK, BLK, 128)

    loads[0].wait()
    merge(1 - core, sib_tx, 0)

    pl.semaphore_wait(barrier, (nrow - 1) + 2 * (ncol - 1))

    def codes_copy(i, source):
        return pltpu.make_async_remote_copy(
            src_ref=codes_tx, dst_ref=codes_rx.at[source],
            send_sem=codes_ssem.at[i], recv_sem=codes_rsem.at[i],
            device_id=(lax.rem(row + i, nrow), col), device_id_type=MESH,
        )

    @pl.loop(1, nrow)
    def _(i):
        codes_copy(i, row).start()

    def pair_copy(i, src, dst):
        return pltpu.make_async_remote_copy(
            src_ref=src, dst_ref=dst, send_sem=pair_ssem.at[i], recv_sem=pair_rsem.at[i],
            device_id=(sib, col), device_id_type=MESH,
        )

    sib_copy = pair_copy(0, sib_tx, sib_rx)
    sib_copy.start()
    merge(core, local, core * SLOTS_BLK)

    @pl.loop(1, nrow)
    def _(i):
        codes_copy(i, lax.rem(row + nrow - i, nrow)).wait_recv()

    missed = plan_routes(codes_rx[...], tbl_v, nz, z, steps)
    tbl_copy = pltpu.make_async_copy(tbl_v, tbl_s, load_sem.at[4])
    tbl_copy.start()
    tbl_copy.wait()
    sib_copy.wait_recv()
    local[pl.ds((1 - core) * SLOTS_BLK, SLOTS_BLK)] = sib_rx[...]

    ahead = lax.rem(row + 2, nrow)
    behind = lax.rem(row + nrow - 2, nrow)

    def hop(t, d):
        return pltpu.make_async_remote_copy(
            src_ref=stage.at[d, t], dst_ref=recv.at[d, t],
            send_sem=hop_ssem.at[d, t], recv_sem=hop_rsem.at[d, t],
            device_id=(behind if d else ahead, col), device_id_type=MESH,
        )

    def take(t):
        for d in range(2):
            hop(t, d).wait_recv()
            local[16 + 2 * t + d] = recv[d, t]

    def put(t):
        for d in range(2):
            stage[d, t] = local[tbl_s[0, 2 * t + d]]
            hop(t, d).start()

    for t in range(DELAY):
        put(t)

    @pl.loop(DELAY, steps)
    def _(t):
        take(t - DELAY)
        put(t)

    for t in range(steps - DELAY, steps):
        take(t)

    for j in range(OWN):
        fin_tx[j] = local[tbl_s[2, OWN * (1 - core) + j]]
    fin_copy = pair_copy(1, fin_tx, fin_rx)
    fin_copy.start()
    for j in range(OWN):
        owned[core, j * BLK:(j + 1) * BLK] = local[tbl_s[2, OWN * core + j]]
    nb_tx[...] = jnp.where(row8 == 2, missed, 0)
    nb_tx[0:OWN, 0:nb_ref.shape[1]] = nb_ref[...]

    def nb_copy(i, source):
        return pltpu.make_async_remote_copy(
            src_ref=nb_tx, dst_ref=nb_rx.at[source],
            send_sem=nb_ssem.at[i], recv_sem=nb_rsem.at[i],
            device_id=(row, lax.rem(col + i, ncol)), device_id_type=MESH,
        )

    nb_rx[col] = nb_tx[...]

    @pl.loop(1, ncol)
    def _(i):
        nb_copy(i, col).start()

    for load in loads[1:]:
        load.wait()
    fin_copy.wait_recv()
    for j in range(OWN):
        owned[1 - core, j * BLK:(j + 1) * BLK] = fin_rx[j]
    left, right = owned[0], owned[1]

    def project(i):
        return (
            jnp.dot(left, wts[i, :half], preferred_element_type=jnp.float32)
            + jnp.dot(right, wts[i, half:], preferred_element_type=jnp.float32)
        ).astype(jnp.bfloat16)

    query, key, value = project(0), project(1), project(2)
    kv_rows = OWN * BLK
    for h in range(heads):
        cols = slice(h * HD, (h + 1) * HD)
        packed = jnp.concatenate([key[:, cols], value[:, cols]], axis=1)
        for j in range(OWN):
            q = query[j * BLK:(j + 1) * BLK, cols]
            msg_tx[OWN * h + j, 0:kv_rows] = packed
            msg_tx[OWN * h + j, kv_rows:kv_rows + BLK // 2] = jnp.concatenate(
                [q[: BLK // 2], q[BLK // 2:]], axis=1
            )

    def msg_copy(i, source):
        other = lax.rem(col + i, ncol)
        return pltpu.make_async_remote_copy(
            src_ref=msg_tx.at[other], dst_ref=msg_rx.at[source],
            send_sem=msg_ssem.at[i], recv_sem=msg_rsem.at[i],
            device_id=(row, other), device_id_type=MESH,
        )

    @pl.loop(1, ncol)
    def _(i):
        msg_copy(i, col).start()

    msg_rx[col] = msg_tx[col]

    def keep(source):
        pairs[pl.ds(OWN * source, OWN)] = msg_rx[source, 0:kv_rows].reshape(OWN, BLK, 128)

    keep(col)
    onehot_t[...] = onehot[...].T

    @pl.loop(1, ncol)
    def _(i):
        nb_copy(i, lax.rem(col + ncol - i, ncol)).wait_recv()

    nb_load = pltpu.make_async_copy(nb_rx, nb_s, load_sem.at[5])
    nb_load.start()
    flag_ref[...] = jnp.max(jnp.where(row8[None] == 2, nb_rx[...], 0), axis=0)
    nb_load.wait()

    @pl.loop(1, ncol)
    def _(i):
        source = lax.rem(col + ncol - i, ncol)
        msg_copy(i, source).wait_recv()
        keep(source)

    slot_q = lax.rem(col, OWN)
    to_core = col // half_col
    here = to_core == core
    low = lax.broadcasted_iota(jnp.int32, (BLK // 2, 128), 1) < HD
    factor = math.log2(math.e) / math.sqrt(HD)
    nb_count = nb_ref.shape[1]

    def att_copy(i):
        other = lax.rem(col + i, ncol)
        return pltpu.make_async_remote_copy(
            src_ref=att_tx.at[other],
            dst_ref=att_rx.at[core * half_col + lax.rem(col, half_col)],
            send_sem=att_ssem.at[i],
            recv_sem=att_rsem.at[core * half_col + lax.rem(col, half_col)],
            device_id=(2 * z + to_core, other), device_id_type=MESH,
        )

    @pl.loop(1, ncol + 1)
    def _(i):
        other = lax.rem(col + i, ncol)
        q2 = msg_rx[other, kv_rows:kv_rows + BLK // 2].astype(jnp.float32)
        q = jnp.concatenate(
            [jnp.where(low, q2, 0.0), jnp.where(low, pltpu.roll(q2, HD, 1), 0.0)], axis=0
        ).astype(jnp.bfloat16)
        tiles = []
        for n in range(nb_count):
            cand = nb_s[other, slot_q, n]
            tiles.append(pairs[cand])
        kv = jnp.concatenate(tiles, axis=0)
        score = lax.dot_general(
            q, kv, (((1,), (1,)), ((), ())), preferred_element_type=jnp.float32
        )
        top = jnp.max(score, axis=1, keepdims=True)
        prob = jnp.exp2((score - top) * factor)
        total = jnp.sum(prob, axis=1, keepdims=True)
        mix = jnp.dot(prob.astype(jnp.bfloat16), kv, preferred_element_type=jnp.float32) / total
        upper, lower = mix[: BLK // 2], mix[BLK // 2:]
        att_tx[other] = jnp.where(low, pltpu.roll(upper, HD, 1), lower).astype(jnp.bfloat16)

        @pl.when(jnp.logical_or(i < ncol, jnp.logical_not(here)))
        def _():
            att_copy(i).start()

    @pl.when(here)
    def _():
        att_rx[core * half_col + lax.rem(col, half_col)] = att_tx[col]

    def att_wait(i):
        pltpu.make_async_remote_copy(
            src_ref=att_tx.at[0], dst_ref=att_rx.at[i],
            send_sem=att_ssem.at[0], recv_sem=att_rsem.at[i],
            device_id=(row, col), device_id_type=MESH,
        ).wait_recv()

    @pl.loop(0, ncol)
    def _(i):
        own_turn = jnp.logical_and(here, i == core * half_col + lax.rem(col, half_col))

        @pl.when(jnp.logical_not(own_turn))
        def _():
            att_wait(i)

    for k in range(2):
        for j in range(OWN):
            for p in range(hh // 2):
                a = att_rx[k * half_col + (2 * p) * OWN + j].astype(jnp.float32)
                b = att_rx[k * half_col + (2 * p + 1) * OWN + j].astype(jnp.float32)
                cols = slice(p * 128, (p + 1) * 128)
                to = 2 * steps + k * OWN + j
                home[to, 0:BLK // 2, cols] = jnp.where(low, a, pltpu.roll(b, HD, 1)).astype(
                    jnp.bfloat16
                )
                home[to, BLK // 2:BLK, cols] = jnp.where(low, pltpu.roll(a, HD, 1), b).astype(
                    jnp.bfloat16
                )

    def ret(t, d):
        return pltpu.make_async_remote_copy(
            src_ref=ret_stage.at[d, t], dst_ref=ret_recv.at[d, t],
            send_sem=ret_ssem.at[d, t], recv_sem=ret_rsem.at[d, t],
            device_id=(ahead if d else behind, col), device_id_type=MESH,
        )

    def ret_take(t):
        for d in range(2):
            ret(t, d).wait_recv()
            home[2 * t + d] = ret_recv[d, t]

    def ret_put(t):
        for d in range(2):
            ret_stage[d, t] = home[tbl_s[1, 16 + 2 * t + d]]
            ret(t, d).start()

    for t in range(DELAY):
        ret_put(steps - 1 - t)

    @pl.loop(DELAY, steps)
    def _(s):
        ret_take(steps - 1 - s + DELAY)
        ret_put(steps - 1 - s)

    for t in reversed(range(DELAY)):
        ret_take(t)

    for b in range(SLOTS_BLK):
        ret_tx[b] = home[tbl_s[1, (1 - core) * SLOTS_BLK + b]]
    ret_copy = pair_copy(2, ret_tx, ret_rx)
    ret_copy.start()
    mine = jnp.concatenate([home[tbl_s[1, core * SLOTS_BLK + b]] for b in range(SLOTS_BLK)], axis=0)
    hot_t = onehot_t[...]
    out_ref[:, pl.ds(pl.multiple_of(core * hw, 128), hw)] = jnp.dot(
        hot_t, mine, preferred_element_type=jnp.float32
    ).astype(jnp.bfloat16)
    ret_copy.wait_recv()
    out_ref[:, pl.ds(pl.multiple_of((1 - core) * hw, 128), hw)] = jnp.dot(
        hot_t, ret_rx[...].reshape(slots, hw), preferred_element_type=jnp.float32
    ).astype(jnp.bfloat16)

    sib_copy.wait_send()
    fin_copy.wait_send()
    ret_copy.wait_send()

    @pl.loop(1, nrow)
    def _(i):
        codes_copy(i, row).wait_send()

    @pl.loop(1, ncol)
    def _(i):
        nb_copy(i, col).wait_send()
        msg_copy(i, col).wait_send()

    @pl.loop(1, ncol + 1)
    def _(i):
        @pl.when(jnp.logical_or(i < ncol, jnp.logical_not(here)))
        def _():
            att_copy(i).wait_send()

    @pl.loop(0, steps)
    def _(t):
        for d in range(2):
            hop(t, d).wait_send()
            ret(t, d).wait_send()


def routed(tokens, merge_map, block_owner, neighbours, w_query, w_key, w_value):
    nrow, ncol = lax.axis_size("row"), lax.axis_size("col")
    count, width = tokens.shape
    head_width = w_query.shape[1]
    heads = head_width // HD
    half, hw = width // 2, head_width // 2
    bf, i32 = jnp.bfloat16, jnp.int32
    places = 16 + 2 * STEPS
    hbm = pl.BlockSpec(memory_space=pl.ANY)
    vmem = pl.BlockSpec(memory_space=pltpu.VMEM)
    smem = pl.BlockSpec(memory_space=pltpu.SMEM)
    dma = pltpu.SemaphoreType.DMA
    msg_rows = OWN * BLK + BLK // 2
    slots = SLOTS_BLK * BLK
    scratch = [
        pltpu.VMEM((count, width), bf),
        pltpu.VMEM((3, width, head_width), bf),
        pltpu.VMEM((slots, count), bf),
        pltpu.VMEM((count, slots), bf),
        pltpu.VMEM((8, 128), i32),
        pltpu.VMEM((nrow, 8, 128), i32),
        pltpu.VMEM((8, 128), i32),
        pltpu.SMEM((8, 128), i32),
        pltpu.VMEM((places, BLK, half), bf),
        pltpu.VMEM((SLOTS_BLK, BLK, half), bf),
        pltpu.VMEM((SLOTS_BLK, BLK, half), bf),
        pltpu.VMEM((2, STEPS, BLK, half), bf),
        pltpu.VMEM((2, STEPS, BLK, half), bf),
        pltpu.VMEM((OWN, BLK, half), bf),
        pltpu.VMEM((OWN, BLK, half), bf),
        pltpu.VMEM((2, OWN * BLK, half), bf),
        pltpu.VMEM((ncol, msg_rows, 128), bf),
        pltpu.VMEM((ncol, msg_rows, 128), bf),
        pltpu.VMEM((OWN * ncol, BLK, 128), bf),
        pltpu.VMEM((8, 128), i32),
        pltpu.VMEM((ncol, 8, 128), i32),
        pltpu.SMEM((ncol, 8, 128), i32),
        pltpu.VMEM((ncol, BLK // 2, 128), bf),
        pltpu.VMEM((ncol, BLK // 2, 128), bf),
        pltpu.VMEM((2 * STEPS + 2 * OWN, BLK, hw), bf),
        pltpu.VMEM((2, STEPS, BLK, hw), bf),
        pltpu.VMEM((2, STEPS, BLK, hw), bf),
        pltpu.VMEM((SLOTS_BLK, BLK, hw), bf),
        pltpu.VMEM((SLOTS_BLK, BLK, hw), bf),
        dma((6,)),
        dma((nrow,)), dma((nrow,)),
        dma((3,)), dma((3,)),
        dma((2, STEPS)), dma((2, STEPS)),
        dma((ncol,)), dma((ncol,)),
        dma((ncol,)), dma((ncol,)),
        dma((ncol + 1,)), dma((ncol,)),
        dma((2, STEPS)), dma((2, STEPS)),
    ]
    return pl.pallas_call(
        functools.partial(kernel, (nrow, ncol, heads, width, STEPS)),
        out_shape=(
            jax.ShapeDtypeStruct((count, head_width), bf),
            jax.ShapeDtypeStruct((8, 128), i32),
        ),
        in_specs=[hbm, vmem, smem, vmem, hbm, hbm, hbm],
        out_specs=(vmem, vmem),
        scratch_shapes=scratch,
        compiler_params=pltpu.CompilerParams(
            collective_id=0, has_side_effects=True, vmem_limit_bytes=56 * 1024 * 1024
        ),
    )(tokens, merge_map.reshape(1, count), block_owner, neighbours, w_query, w_key, w_value)


def program(*args):
    out, missed = routed(*args)
    return lax.cond(missed[2, 0] > 0, lambda: on_device(*args), lambda: out)


def solution(mesh):
    in_specs = (
        P(("row", "col"), None),
        P(("row", "col")),
        P(("row", "col"), None),
        P(("row", "col"), None),
        P(),
        P(),
        P(),
    )
    out_specs = P(("row", "col"), None)
    return jax.shard_map(
        program, mesh=mesh, in_specs=in_specs, out_specs=out_specs, check_vma=False
    )
```

```python
import functools
import math

import jax
import jax.numpy as jnp
from jax import lax
from jax.experimental import pallas as pl
from jax.experimental.pallas import tpu as pltpu
from jax.sharding import PartitionSpec as P

HD = 64
BLK = 64
OWN = 2
SLOTS_BLK = 8
PARTS = 2
PART = BLK // PARTS
MESH = pl.DeviceIdType.MESH
DIST = (1, 2, 1, 1, 2, 1, 1, 2, 1, 1, 1, 2, 2, 1, 1, 1)
NEED = (0, 0, 0, 0, 1, 2, 3, 5, 7, 7, 8, 9, 11, 12, 13, 14)
FIXED_LAG = 3


def plan_start(place, nz, rows):
    shape = (rows, 128)
    place = jnp.broadcast_to(place, shape)
    lane = lax.broadcasted_iota(jnp.int32, shape, 1)
    valid = place > 0
    place = jnp.where(valid, place - 1, 0)
    pos = place >> 4
    fwd = ((lane >> 2) - pos) & (nz - 1)
    half = nz // 2
    right = (fwd < half) | ((fwd == half) & ((lane & 1) == 0))
    rem = jnp.where(valid, jnp.where(right, fwd, nz - fwd), 0)
    return lane, pos, jnp.where(right, 0, 1), rem, place & 15


def plan_first(place, tbl_v, nz):
    lane, _, way, rem, loc = plan_start(place, nz, 8)
    row = lax.broadcasted_iota(jnp.int32, (8, 128), 0)
    send = jnp.zeros((8, 128), jnp.int32)
    left = jnp.where(way == row, rem, 0)
    for t in range(len(DIST)):
        if NEED[t] == 0:
            key = jnp.where(left >= DIST[t], left * 128 + lane + 1, 0)
            best = jnp.max(key, axis=1, keepdims=True)
            pick = (key == best) & (key > 0)
            own = jnp.sum(jnp.where(pick, loc, 0), axis=1, keepdims=True)
            send = jnp.where(lane == t, own, send)
            left = jnp.where(pick, 0, left)
    tbl_v[...] = send


def plan_routes(place, tbl_v, nz, z, slots, fixed):
    rows = max(2 * nz, 8)
    shape = (rows, 128)
    lane, pos, way, rem, loc = plan_start(place, nz, rows)
    row = lax.broadcasted_iota(jnp.int32, shape, 0)
    row_way = jnp.where(row >= nz, 1, 0)
    at = pos + nz * way
    sign = 1 - 2 * way
    ready = jnp.zeros(shape, jnp.int32)
    send = jnp.zeros(shape, jnp.int32)
    back = jnp.full(shape, -1, jnp.int32)
    for t, (dist, need) in enumerate(slots):
        go = (at == row) & (rem >= dist) & (ready <= need)
        if fixed:
            go = go & (rem == nz // 2 - t // 4) & ((lane & 3) == t % 4)
        key = jnp.where(go, rem * 128 + lane + 1, 0)
        best = jnp.max(key, axis=1, keepdims=True)
        pick = jnp.where(key == best, jnp.minimum(key, 1), 0)
        moved = jnp.broadcast_to(jnp.max(pick, axis=0, keepdims=True), shape) > 0
        own = jnp.broadcast_to(jnp.sum(pick * (loc + 1), axis=1, keepdims=True), shape)
        send = jnp.where(lane == t, own, send)
        back = jnp.where(lane == own - 1, 2 * t + row_way, back)
        at = jnp.where(moved, (at & nz) | ((at + dist * sign) & (nz - 1)), at)
        rem = jnp.where(moved, rem - dist, rem)
        ready = jnp.where(moved, t + 1, ready)
        loc = jnp.where(moved, 16 + 2 * t + way, loc)
    count = len(slots)

    def line(value):
        return jnp.broadcast_to(value, (8, 128))

    right = line(jnp.sum(jnp.where(row == z, send, 0), axis=0, keepdims=True))
    left = line(jnp.sum(jnp.where(row == z + nz, send, 0), axis=0, keepdims=True))
    here = (row == z) | (row == z + nz)
    home = line(jnp.max(jnp.where(here, back, -1), axis=0, keepdims=True))
    home = jnp.where(home < 0, 2 * count, home)
    lane8 = lane[:8]
    final = jnp.zeros((8, 128), jnp.int32)
    for i in range(2 * OWN):
        end = jnp.sum(jnp.where(lane == 2 * OWN * z + i, loc, 0), axis=1, keepdims=True)[:8]
        home = jnp.where(lane8 == end, 2 * count + i, home)
        final = jnp.where(lane8 == i, end, final)
    row8 = row[:8]
    table = jnp.where(row8 == 0, jnp.maximum(right - 1, 0), jnp.maximum(left - 1, 0))
    tbl_v[...] = jnp.where(row8 < 2, table, jnp.where(row8 == 2, home, final))
    return line(jnp.max(rem, axis=1, keepdims=True)[:8])


def in_turn(slots, parts, lag, put, take):
    count = len(slots)
    if lag:
        for t in range(lag):
            for h in range(parts):
                put(t, h)

        @pl.loop(lag, count)
        def _(t):
            for h in range(parts):
                take(t - lag, h)
                put(t, h)

        for t in range(count - lag, count):
            for h in range(parts):
                take(t, h)
        return
    done = 0
    for t, need in enumerate(slots):
        for h in range(parts):
            for u in range(done, need):
                take(u, h)
            put(t, h)
        done = max(done, need)
    for u in range(done, count):
        for h in range(parts):
            take(u, h)


def kernel(
    dims,
    tokens_hbm, map_ref, owner_ref, nb_ref, wq_hbm, wk_hbm, wv_hbm,
    out_ref, flag_ref,
    tok, wts, onehot, onehot_t,
    codes_tx, codes_rx, codes_sib, tbl_v, tbl_s, first_v, first_s,
    local_a, local_b, sib_tx, sib_rx, stage, recv, fin_tx, fin_rx, owned,
    msg_tx, msg_rx, pairs, nb_tx, nb_rx, nb_s, miss_tx, miss_rx, miss_s,
    att_tx, att_rx, home, ret_stage, ret_recv, ret_tx, ret_rx,
    load_sem, codes_ssem, codes_rsem, pair_ssem, pair_rsem, hop_ssem, hop_rsem,
    msg_ssem, msg_rsem, nb_ssem, nb_rsem, miss_ssem, miss_rsem, att_ssem, att_rsem,
    ret_ssem, ret_rsem,
):
    nrow, ncol, heads, width, slot_plan, fixed = dims
    nz = nrow // 2
    steps = len(slot_plan)
    local = (local_a, local_b)
    half = width // 2
    hh = heads // 2
    hw = hh * HD
    half_col = ncol // 2
    slots = SLOTS_BLK * BLK
    row = lax.axis_index("row")
    col = lax.axis_index("col")
    z = row // 2
    core = lax.rem(row, 2)
    sib = row + 1 - 2 * core
    barrier = pltpu.get_barrier_semaphore()

    loads = [pltpu.make_async_copy(tokens_hbm, tok, load_sem.at[0])]
    for i, w in enumerate((wq_hbm, wk_hbm, wv_hbm)):
        loads.append(pltpu.make_async_copy(w, wts.at[i], load_sem.at[i + 1]))
    for load in loads:
        load.start()

    @pl.loop(1, nrow)
    def _(i):
        pl.semaphore_signal(
            barrier, inc=1, device_id=(lax.rem(row + i, nrow), col), device_id_type=MESH
        )

    @pl.loop(1, ncol)
    def _(i):
        other = lax.rem(col + i, ncol)
        pl.semaphore_signal(barrier, inc=1, device_id=(row, other), device_id_type=MESH)
        pl.semaphore_signal(barrier, inc=1, device_id=(sib, other), device_id_type=MESH)

    lane8 = lax.broadcasted_iota(jnp.int32, (8, 128), 1)
    row8 = lax.broadcasted_iota(jnp.int32, (8, 128), 0)
    codes = jnp.zeros((8, 128), jnp.int32)
    for b in range(SLOTS_BLK):
        codes = jnp.where((lane8 == owner_ref[0, b]) & (row8 == 0), row * 8 + b + 1, codes)
    codes_tx[...] = codes
    codes_rx[row] = codes

    slot_ids = lax.broadcasted_iota(jnp.int32, (slots, map_ref.shape[1]), 0)
    hot = jnp.where(slot_ids == map_ref[...], 1.0, 0.0).astype(jnp.bfloat16)
    onehot[...] = hot
    count = jnp.dot(
        hot, jnp.ones((map_ref.shape[1], 128), jnp.bfloat16), preferred_element_type=jnp.float32
    )
    share = 1.0 / jnp.maximum(count, 1.0)

    def merge(which, store):
        sums = jnp.dot(
            onehot[...],
            tok[:, pl.ds(pl.multiple_of(which * half, 128), half)],
            preferred_element_type=jnp.float32,
        )
        for i in range(half // 128):
            cols = slice(i * 128, (i + 1) * 128)
            part = (sums[:, cols] * share).astype(jnp.bfloat16)
            store(part.reshape(SLOTS_BLK, BLK, 128), cols)

    loads[0].wait()

    def to_sib(part, cols):
        sib_tx[:, :, cols] = part

    merge(1 - core, to_sib)

    pl.semaphore_wait(barrier, (nrow - 1) + 2 * (ncol - 1))

    def codes_copy(i, source):
        return pltpu.make_async_remote_copy(
            src_ref=codes_tx, dst_ref=codes_rx.at[source],
            send_sem=codes_ssem.at[i], recv_sem=codes_rsem.at[i],
            device_id=(lax.rem(row + i, nrow), col), device_id_type=MESH,
        )

    def pair_copy(i, src, dst):
        return pltpu.make_async_remote_copy(
            src_ref=src, dst_ref=dst, send_sem=pair_ssem.at[i], recv_sem=pair_rsem.at[i],
            device_id=(sib, col), device_id_type=MESH,
        )

    code_copy = pair_copy(3, codes_tx, codes_sib)
    code_copy.start()
    sib_copy = pair_copy(0, sib_tx, sib_rx)
    sib_copy.start()

    @pl.loop(1, nrow)
    def _(i):
        codes_copy(i, row).start()

    def to_own(part, cols):
        for h in range(PARTS):
            local[h][pl.ds(core * SLOTS_BLK, SLOTS_BLK), :, cols] = part[
                :, h * PART:(h + 1) * PART
            ]

    merge(core, to_own)

    def away(t, d):
        far = 2 * (1 if fixed else slot_plan[t][0])
        return lax.rem(row + (nrow - far if d else far), nrow)

    def hop(t, d, h):
        return pltpu.make_async_remote_copy(
            src_ref=stage.at[h, d, t], dst_ref=recv.at[h, d, t],
            send_sem=hop_ssem.at[h, d, t], recv_sem=hop_rsem.at[h, d, t],
            device_id=(away(t, d), col), device_id_type=MESH,
        )

    def take(t, h):
        for d in range(2):
            hop(t, d, h).wait_recv()
            local[h][16 + 2 * t + d] = recv[h, d, t]

    def put(t, h, table=tbl_s):
        for d in range(2):
            stage[h, d, t] = local[h][table[d, t]]
            hop(t, d, h).start()

    def sib_arrived():
        sib_copy.wait_recv()
        for h in range(PARTS):
            local[h][pl.ds((1 - core) * SLOTS_BLK, SLOTS_BLK)] = sib_rx[
                :, h * PART:(h + 1) * PART
            ]

    early = 0 if fixed else sum(need == 0 for _, need in slot_plan)
    code_copy.wait_recv()
    if early:
        near = jnp.sum(codes_tx[...] + codes_sib[...], axis=0, keepdims=True)
        plan_first(near, first_v, nz)
        first_copy = pltpu.make_async_copy(first_v, first_s, load_sem.at[6])
        first_copy.start()
        sib_arrived()
        first_copy.wait()
        for t in range(early):
            for h in range(PARTS):
                put(t, h, first_s)

    nb_tx[...] = jnp.zeros((8, 128), jnp.int32)
    nb_tx[0:OWN, 0:nb_ref.shape[1]] = nb_ref[...]

    def plane_copy(i, source, src, dst, ssem, rsem):
        return pltpu.make_async_remote_copy(
            src_ref=src, dst_ref=dst.at[source], send_sem=ssem.at[i], recv_sem=rsem.at[i],
            device_id=(row, lax.rem(col + i, ncol)), device_id_type=MESH,
        )

    def nb_copy(i, source):
        return plane_copy(i, source, nb_tx, nb_rx, nb_ssem, nb_rsem)

    def miss_copy(i, source):
        return plane_copy(i, source, miss_tx, miss_rx, miss_ssem, miss_rsem)

    nb_rx[col] = nb_tx[...]

    @pl.loop(1, ncol)
    def _(i):
        nb_copy(i, col).start()

    @pl.loop(1, nrow)
    def _(i):
        codes_copy(i, lax.rem(row + nrow - i, nrow)).wait_recv()

    place = jnp.sum(jnp.sum(codes_rx[...], axis=0), axis=0, keepdims=True)
    miss_tx[...] = plan_routes(place, tbl_v, nz, z, slot_plan, fixed)
    tbl_copy = pltpu.make_async_copy(tbl_v, tbl_s, load_sem.at[4])
    tbl_copy.start()
    tbl_copy.wait()
    if not early:
        sib_arrived()
    needs = [need for _, need in slot_plan]

    def put_late(t, h):
        if fixed or t >= early:
            put(t, h)

    in_turn(needs, PARTS, FIXED_LAG if fixed else 0, put_late, take)

    for j in range(OWN):
        for h in range(PARTS):
            fin_tx[j, h * PART:(h + 1) * PART] = local[h][tbl_s[3, OWN * (1 - core) + j]]
    fin_copy = pair_copy(1, fin_tx, fin_rx)
    fin_copy.start()
    for j in range(OWN):
        for h in range(PARTS):
            base = j * BLK + h * PART
            owned[core, base:base + PART] = local[h][tbl_s[3, OWN * core + j]]
    for load in loads[1:]:
        load.wait()
    fin_copy.wait_recv()
    for j in range(OWN):
        owned[1 - core, j * BLK:(j + 1) * BLK] = fin_rx[j]
    left, right = owned[0], owned[1]

    def project(i):
        return (
            jnp.dot(left, wts[i, :half], preferred_element_type=jnp.float32)
            + jnp.dot(right, wts[i, half:], preferred_element_type=jnp.float32)
        ).astype(jnp.bfloat16)

    query, key, value = project(0), project(1), project(2)
    kv_rows = OWN * BLK
    for h in range(heads):
        cols = slice(h * HD, (h + 1) * HD)
        packed = jnp.concatenate([key[:, cols], value[:, cols]], axis=1)
        for j in range(OWN):
            q = query[j * BLK:(j + 1) * BLK, cols]
            msg_tx[OWN * h + j, 0:kv_rows] = packed
            msg_tx[OWN * h + j, kv_rows:kv_rows + BLK // 2] = jnp.concatenate(
                [q[: BLK // 2], q[BLK // 2:]], axis=1
            )

    def msg_copy(i, source):
        other = lax.rem(col + i, ncol)
        return pltpu.make_async_remote_copy(
            src_ref=msg_tx.at[other], dst_ref=msg_rx.at[source],
            send_sem=msg_ssem.at[i], recv_sem=msg_rsem.at[i],
            device_id=(row, other), device_id_type=MESH,
        )

    @pl.loop(1, ncol)
    def _(i):
        msg_copy(i, col).start()

    msg_rx[col] = msg_tx[col]

    def keep(source):
        pairs[pl.ds(OWN * source, OWN)] = msg_rx[source, 0:kv_rows].reshape(OWN, BLK, 128)

    keep(col)
    onehot_t[...] = onehot[...].T

    @pl.loop(1, ncol)
    def _(i):
        nb_copy(i, lax.rem(col + ncol - i, ncol)).wait_recv()

    nb_load = pltpu.make_async_copy(nb_rx, nb_s, load_sem.at[5])
    nb_load.start()
    nb_load.wait()

    @pl.loop(1, ncol)
    def _(i):
        source = lax.rem(col + ncol - i, ncol)
        msg_copy(i, source).wait_recv()
        keep(source)

    slot_q = lax.rem(col, OWN)
    to_core = col // half_col
    here = to_core == core
    low = lax.broadcasted_iota(jnp.int32, (BLK // 2, 128), 1) < HD
    factor = math.log2(math.e) / math.sqrt(HD)
    nb_count = nb_ref.shape[1]

    def att_copy(i):
        other = lax.rem(col + i, ncol)
        return pltpu.make_async_remote_copy(
            src_ref=att_tx.at[other],
            dst_ref=att_rx.at[core * half_col + lax.rem(col, half_col)],
            send_sem=att_ssem.at[i],
            recv_sem=att_rsem.at[core * half_col + lax.rem(col, half_col)],
            device_id=(2 * z + to_core, other), device_id_type=MESH,
        )

    @pl.loop(1, ncol + 1)
    def _(i):
        other = lax.rem(col + i, ncol)
        q2 = msg_rx[other, kv_rows:kv_rows + BLK // 2].astype(jnp.float32)
        q = jnp.concatenate(
            [jnp.where(low, q2, 0.0), jnp.where(low, pltpu.roll(q2, HD, 1), 0.0)], axis=0
        ).astype(jnp.bfloat16)
        tiles = []
        for n in range(nb_count):
            cand = nb_s[other, slot_q, n]
            tiles.append(pairs[cand])
        kv = jnp.concatenate(tiles, axis=0)
        score = lax.dot_general(
            q, kv, (((1,), (1,)), ((), ())), preferred_element_type=jnp.float32
        )
        top = jnp.max(score, axis=1, keepdims=True)
        prob = jnp.exp2((score - top) * factor)
        total = jnp.sum(prob, axis=1, keepdims=True)
        mix = jnp.dot(prob.astype(jnp.bfloat16), kv, preferred_element_type=jnp.float32) / total
        upper, lower = mix[: BLK // 2], mix[BLK // 2:]
        att_tx[other] = jnp.where(low, pltpu.roll(upper, HD, 1), lower).astype(jnp.bfloat16)

        @pl.when(jnp.logical_or(i < ncol, jnp.logical_not(here)))
        def _():
            att_copy(i).start()

    @pl.when(here)
    def _():
        att_rx[core * half_col + lax.rem(col, half_col)] = att_tx[col]

    def att_wait(i):
        pltpu.make_async_remote_copy(
            src_ref=att_tx.at[0], dst_ref=att_rx.at[i],
            send_sem=att_ssem.at[0], recv_sem=att_rsem.at[i],
            device_id=(row, col), device_id_type=MESH,
        ).wait_recv()

    @pl.loop(0, ncol)
    def _(i):
        own_turn = jnp.logical_and(here, i == core * half_col + lax.rem(col, half_col))

        @pl.when(jnp.logical_not(own_turn))
        def _():
            att_wait(i)

    for k in range(2):
        for j in range(OWN):
            for p in range(hh // 2):
                a = att_rx[k * half_col + (2 * p) * OWN + j].astype(jnp.float32)
                b = att_rx[k * half_col + (2 * p + 1) * OWN + j].astype(jnp.float32)
                cols = slice(p * 128, (p + 1) * 128)
                to = 2 * steps + k * OWN + j
                home[to, 0:BLK // 2, cols] = jnp.where(low, a, pltpu.roll(b, HD, 1)).astype(
                    jnp.bfloat16
                )
                home[to, BLK // 2:BLK, cols] = jnp.where(low, pltpu.roll(a, HD, 1), b).astype(
                    jnp.bfloat16
                )

    def ret(t, d):
        return pltpu.make_async_remote_copy(
            src_ref=ret_stage.at[d, t], dst_ref=ret_recv.at[d, t],
            send_sem=ret_ssem.at[d, t], recv_sem=ret_rsem.at[d, t],
            device_id=(away(t, 1 - d), col), device_id_type=MESH,
        )

    def ret_take(s, _):
        t = steps - 1 - s
        for d in range(2):
            ret(t, d).wait_recv()
            home[2 * t + d] = ret_recv[d, t]

    def ret_put(s, _):
        t = steps - 1 - s
        for d in range(2):
            ret_stage[d, t] = home[tbl_s[2, 16 + 2 * t + d]]
            ret(t, d).start()
        if not fixed and s == 1:
            tell()

    def tell():
        @pl.loop(1, ncol)
        def _(i):
            miss_copy(i, col).start()

    if fixed:
        tell()
    ret_needs = [
        steps - min([u for u in range(steps) if needs[u] > t], default=steps)
        for t in reversed(range(steps))
    ]
    in_turn(ret_needs, 1, FIXED_LAG if fixed else 0, ret_put, ret_take)

    for b in range(SLOTS_BLK):
        ret_tx[b] = home[tbl_s[2, (1 - core) * SLOTS_BLK + b]]
    ret_copy = pair_copy(2, ret_tx, ret_rx)
    ret_copy.start()
    mine = jnp.concatenate([home[tbl_s[2, core * SLOTS_BLK + b]] for b in range(SLOTS_BLK)], axis=0)
    hot_t = onehot_t[...]
    out_ref[:, pl.ds(pl.multiple_of(core * hw, 128), hw)] = jnp.dot(
        hot_t, mine, preferred_element_type=jnp.float32
    ).astype(jnp.bfloat16)
    miss_rx[col] = miss_tx[...]

    @pl.loop(1, ncol)
    def _(i):
        miss_copy(i, lax.rem(col + ncol - i, ncol)).wait_recv()

    first_v[...] = jnp.max(miss_rx[...], axis=0)
    miss_load = pltpu.make_async_copy(first_v, miss_s, load_sem.at[7])
    miss_load.start()
    miss_load.wait()
    flag_ref[0] = miss_s[0, 0]
    ret_copy.wait_recv()
    out_ref[:, pl.ds(pl.multiple_of((1 - core) * hw, 128), hw)] = jnp.dot(
        hot_t, ret_rx[...].reshape(slots, hw), preferred_element_type=jnp.float32
    ).astype(jnp.bfloat16)

    code_copy.wait_send()
    sib_copy.wait_send()
    fin_copy.wait_send()
    ret_copy.wait_send()

    @pl.loop(1, nrow)
    def _(i):
        codes_copy(i, row).wait_send()

    @pl.loop(1, ncol)
    def _(i):
        nb_copy(i, col).wait_send()
        miss_copy(i, col).wait_send()
        msg_copy(i, col).wait_send()

    @pl.loop(1, ncol + 1)
    def _(i):
        @pl.when(jnp.logical_or(i < ncol, jnp.logical_not(here)))
        def _():
            att_copy(i).wait_send()

    def sent(t):
        for d in range(2):
            for h in range(PARTS):
                hop(t, d, h).wait_send()
            ret(t, d).wait_send()

    if fixed:
        pl.loop(0, steps)(sent)
    else:
        for t in range(steps):
            sent(t)


def routed(fixed, tokens, merge_map, block_owner, neighbours, w_query, w_key, w_value):
    nrow, ncol = lax.axis_size("row"), lax.axis_size("col")
    count, width = tokens.shape
    head_width = w_query.shape[1]
    heads = head_width // HD
    half, hw = width // 2, head_width // 2
    bf, i32 = jnp.bfloat16, jnp.int32
    if fixed:
        slot_plan = tuple((1, max(0, t - FIXED_LAG + 1)) for t in range(nrow))
    else:
        slot_plan = tuple(zip(DIST, NEED))
    steps = len(slot_plan)
    places = 16 + 2 * steps
    hbm = pl.BlockSpec(memory_space=pl.ANY)
    vmem = pl.BlockSpec(memory_space=pltpu.VMEM)
    smem = pl.BlockSpec(memory_space=pltpu.SMEM)
    dma = pltpu.SemaphoreType.DMA
    msg_rows = OWN * BLK + BLK // 2
    slots = SLOTS_BLK * BLK
    scratch = [
        pltpu.VMEM((count, width), bf),
        pltpu.VMEM((3, width, head_width), bf),
        pltpu.VMEM((slots, count), bf),
        pltpu.VMEM((count, slots), bf),
        pltpu.VMEM((8, 128), i32),
        pltpu.VMEM((nrow, 8, 128), i32),
        pltpu.VMEM((8, 128), i32),
        pltpu.VMEM((8, 128), i32),
        pltpu.SMEM((8, 128), i32),
        pltpu.VMEM((8, 128), i32),
        pltpu.SMEM((8, 128), i32),
        pltpu.VMEM((places, PART, half), bf),
        pltpu.VMEM((places, PART, half), bf),
        pltpu.VMEM((SLOTS_BLK, BLK, half), bf),
        pltpu.VMEM((SLOTS_BLK, BLK, half), bf),
        pltpu.VMEM((PARTS, 2, steps, PART, half), bf),
        pltpu.VMEM((PARTS, 2, steps, PART, half), bf),
        pltpu.VMEM((OWN, BLK, half), bf),
        pltpu.VMEM((OWN, BLK, half), bf),
        pltpu.VMEM((2, OWN * BLK, half), bf),
        pltpu.VMEM((ncol, msg_rows, 128), bf),
        pltpu.VMEM((ncol, msg_rows, 128), bf),
        pltpu.VMEM((OWN * ncol, BLK, 128), bf),
        pltpu.VMEM((8, 128), i32),
        pltpu.VMEM((ncol, 8, 128), i32),
        pltpu.SMEM((ncol, 8, 128), i32),
        pltpu.VMEM((8, 128), i32),
        pltpu.VMEM((ncol, 8, 128), i32),
        pltpu.SMEM((8, 128), i32),
        pltpu.VMEM((ncol, BLK // 2, 128), bf),
        pltpu.VMEM((ncol, BLK // 2, 128), bf),
        pltpu.VMEM((2 * steps + 2 * OWN, BLK, hw), bf),
        pltpu.VMEM((2, steps, BLK, hw), bf),
        pltpu.VMEM((2, steps, BLK, hw), bf),
        pltpu.VMEM((SLOTS_BLK, BLK, hw), bf),
        pltpu.VMEM((SLOTS_BLK, BLK, hw), bf),
        dma((8,)),
        dma((nrow,)), dma((nrow,)),
        dma((4,)), dma((4,)),
        dma((PARTS, 2, steps)), dma((PARTS, 2, steps)),
        dma((ncol,)), dma((ncol,)),
        dma((ncol,)), dma((ncol,)),
        dma((ncol,)), dma((ncol,)),
        dma((ncol + 1,)), dma((ncol,)),
        dma((2, steps)), dma((2, steps)),
    ]
    return pl.pallas_call(
        functools.partial(kernel, (nrow, ncol, heads, width, slot_plan, fixed)),
        out_shape=(
            jax.ShapeDtypeStruct((count, head_width), bf),
            jax.ShapeDtypeStruct((1,), i32),
        ),
        in_specs=[hbm, vmem, smem, vmem, hbm, hbm, hbm],
        out_specs=(vmem, smem),
        scratch_shapes=scratch,
        compiler_params=pltpu.CompilerParams(
            collective_id=int(fixed), has_side_effects=True, vmem_limit_bytes=56 * 1024 * 1024
        ),
    )(tokens, merge_map.reshape(1, count), block_owner, neighbours, w_query, w_key, w_value)


def program(*args):
    out, missed = routed(False, *args)
    return lax.cond(missed[0] > 0, lambda: routed(True, *args)[0], lambda: out)


def solution(mesh):
    in_specs = (
        P(("row", "col"), None),
        P(("row", "col")),
        P(("row", "col"), None),
        P(("row", "col"), None),
        P(),
        P(),
        P(),
    )
    out_specs = P(("row", "col"), None)
    return jax.shard_map(
        program, mesh=mesh, in_specs=in_specs, out_specs=out_specs, check_vma=False
    )
```

```python
import functools
import math

import jax
import jax.numpy as jnp
from jax import lax
from jax.experimental import pallas as pl
from jax.experimental.pallas import tpu as pltpu
from jax.sharding import PartitionSpec as P

HD = 64
BLK = 64
OWN = 2
SLOTS_BLK = 8
PARTS = 2
PART = BLK // PARTS
TOGETHER = 4
MESH = pl.DeviceIdType.MESH
DIST = (1, 2, 1, 1, 2, 1, 1, 2, 1, 1, 1, 2, 2, 1, 1, 1)
NEED = (0, 0, 0, 0, 1, 2, 3, 5, 7, 7, 8, 9, 11, 12, 13, 14)
FIXED_LAG = 3


def plan_start(place, nz, rows):
    shape = (rows, 128)
    place = jnp.broadcast_to(place, shape)
    lane = lax.broadcasted_iota(jnp.int32, shape, 1)
    valid = place > 0
    place = jnp.where(valid, place - 1, 0)
    pos = place >> 4
    fwd = ((lane >> 2) - pos) & (nz - 1)
    half = nz // 2
    right = (fwd < half) | ((fwd == half) & ((lane & 1) == 0))
    rem = jnp.where(valid, jnp.where(right, fwd, nz - fwd), 0)
    return lane, pos, jnp.where(right, 0, 1), rem, place & 15


def plan_first(place, tbl_v, nz):
    lane, _, way, rem, loc = plan_start(place, nz, 8)
    row = lax.broadcasted_iota(jnp.int32, (8, 128), 0)
    send = jnp.zeros((8, 128), jnp.int32)
    left = jnp.where(way == row, rem, 0)
    for t in range(len(DIST)):
        if NEED[t] == 0:
            key = jnp.where(left >= DIST[t], left * 128 + lane + 1, 0)
            best = jnp.max(key, axis=1, keepdims=True)
            pick = (key == best) & (key > 0)
            own = jnp.sum(jnp.where(pick, loc, 0), axis=1, keepdims=True)
            send = jnp.where(lane == t, own, send)
            left = jnp.where(pick, 0, left)
    tbl_v[...] = send


def plan_routes(place, tbl_v, nz, z, slots, fixed):
    rows = max(2 * nz, 8)
    shape = (rows, 128)
    lane, pos, way, rem, loc = plan_start(place, nz, rows)
    row = lax.broadcasted_iota(jnp.int32, shape, 0)
    row_way = jnp.where(row >= nz, 1, 0)
    at = pos + nz * way
    sign = 1 - 2 * way
    ready = jnp.zeros(shape, jnp.int32)
    send = jnp.zeros(shape, jnp.int32)
    back = jnp.full(shape, -1, jnp.int32)
    for t, (dist, need) in enumerate(slots):
        go = (at == row) & (rem >= dist) & (ready <= need)
        if fixed:
            go = go & (rem == nz // 2 - t // 4) & ((lane & 3) == t % 4)
        key = jnp.where(go, rem * 128 + lane + 1, 0)
        best = jnp.max(key, axis=1, keepdims=True)
        pick = jnp.where(key == best, jnp.minimum(key, 1), 0)
        moved = jnp.broadcast_to(jnp.max(pick, axis=0, keepdims=True), shape) > 0
        own = jnp.broadcast_to(jnp.sum(pick * (loc + 1), axis=1, keepdims=True), shape)
        send = jnp.where(lane == t, own, send)
        back = jnp.where(lane == own - 1, 2 * t + row_way, back)
        at = jnp.where(moved, (at & nz) | ((at + dist * sign) & (nz - 1)), at)
        rem = jnp.where(moved, rem - dist, rem)
        ready = jnp.where(moved, t + 1, ready)
        loc = jnp.where(moved, 16 + 2 * t + way, loc)
    count = len(slots)

    def line(value):
        return jnp.broadcast_to(value, (8, 128))

    right = line(jnp.sum(jnp.where(row == z, send, 0), axis=0, keepdims=True))
    left = line(jnp.sum(jnp.where(row == z + nz, send, 0), axis=0, keepdims=True))
    here = (row == z) | (row == z + nz)
    home = line(jnp.max(jnp.where(here, back, -1), axis=0, keepdims=True))
    home = jnp.where(home < 0, 2 * count, home)
    lane8 = lane[:8]
    final = jnp.zeros((8, 128), jnp.int32)
    for i in range(2 * OWN):
        end = jnp.sum(jnp.where(lane == 2 * OWN * z + i, loc, 0), axis=1, keepdims=True)[:8]
        home = jnp.where(lane8 == end, 2 * count + i, home)
        final = jnp.where(lane8 == i, end, final)
    row8 = row[:8]
    table = jnp.where(row8 == 0, jnp.maximum(right - 1, 0), jnp.maximum(left - 1, 0))
    tbl_v[...] = jnp.where(row8 < 2, table, jnp.where(row8 == 2, home, final))
    return line(jnp.max(rem, axis=1, keepdims=True)[:8])


def in_turn(slots, parts, lag, put, take):
    count = len(slots)
    if lag:
        for t in range(lag):
            for h in range(parts):
                put(t, h)

        @pl.loop(lag, count)
        def _(t):
            for h in range(parts):
                take(t - lag, h)
                put(t, h)

        for t in range(count - lag, count):
            for h in range(parts):
                take(t, h)
        return
    done = 0
    for t, need in enumerate(slots):
        for h in range(parts):
            for u in range(done, need):
                take(u, h)
            put(t, h)
        done = max(done, need)
    for u in range(done, count):
        for h in range(parts):
            take(u, h)


def kernel(
    dims,
    tokens_hbm, map_hbm, owner_hbm, nb_hbm, wq_hbm, wk_hbm, wv_hbm,
    out_ref, flag_ref,
    tok, wts, map_ref, owner_ref, nb_ref, onehot, onehot_t,
    codes_tx, codes_rx, codes_sib, tbl_v, tbl_s, first_v, first_s,
    sib_tx, sib_rx, stage, recv, fin_tx, fin_rx, owned,
    msg_tx, msg_rx, pairs, nb_tx, nb_rx, nb_s, miss_tx, miss_rx, miss_s,
    att_tx, att_rx, ret_stage, ret_recv, ret_tx, ret_rx,
    load_sem, codes_ssem, codes_rsem, pair_ssem, pair_rsem, hop_ssem, hop_rsem,
    msg_ssem, msg_rsem, nb_ssem, nb_rsem, miss_ssem, miss_rsem, att_ssem, att_rsem,
    ret_ssem, ret_rsem, *kept,
):
    nrow, ncol, heads, width, slot_plan, fixed = dims
    nz = nrow // 2
    steps = len(slot_plan)
    local, home = kept[:PARTS], kept[PARTS:]
    side = math.isqrt(ncol)
    half = width // 2
    hh = heads // 2
    hw = hh * HD
    half_col = ncol // 2
    slots = SLOTS_BLK * BLK
    row = lax.axis_index("row")
    col = lax.axis_index("col")
    z = row // 2
    core = lax.rem(row, 2)
    sib = row + 1 - 2 * core
    barrier = pltpu.get_barrier_semaphore()

    small = [
        pltpu.make_async_copy(src, dst, load_sem.at[8 + i])
        for i, (src, dst) in enumerate(
            ((owner_hbm, owner_ref), (map_hbm, map_ref), (nb_hbm, nb_ref))
        )
    ]
    for copy in small:
        copy.start()
    loads = [pltpu.make_async_copy(tokens_hbm, tok, load_sem.at[0])]
    for i, w in enumerate((wq_hbm, wk_hbm, wv_hbm)):
        loads.append(pltpu.make_async_copy(w, wts.at[i], load_sem.at[i + 1]))
    for load in loads:
        load.start()

    def ring(i):
        return nrow // 2 + ((i + 1) // 2) * (1 - 2 * lax.rem(i, 2))

    def plane(i, sign=1):
        dx, dy = (0x36 >> (2 * (i // side))) & 3, (0x36 >> (2 * lax.rem(i, side))) & 3
        x = lax.rem(col // side + side + sign * dx, side)
        y = lax.rem(lax.rem(col, side) + side + sign * dy, side)
        return x * side + y

    @pl.loop(0, nrow - 1)
    def _(i):
        pl.semaphore_signal(
            barrier, inc=1, device_id=(lax.rem(row + ring(i), nrow), col), device_id_type=MESH
        )

    @pl.loop(0, ncol - 1)
    def _(i):
        other = plane(i)
        pl.semaphore_signal(barrier, inc=1, device_id=(row, other), device_id_type=MESH)
        pl.semaphore_signal(barrier, inc=1, device_id=(sib, other), device_id_type=MESH)

    for copy in small:
        copy.wait()

    lane8 = lax.broadcasted_iota(jnp.int32, (8, 128), 1)
    row8 = lax.broadcasted_iota(jnp.int32, (8, 128), 0)
    codes = jnp.zeros((8, 128), jnp.int32)
    for b in range(SLOTS_BLK):
        codes = jnp.where((lane8 == owner_ref[0, b]) & (row8 == 0), row * 8 + b + 1, codes)
    codes_tx[...] = codes
    codes_rx[row] = codes

    slot_ids = lax.broadcasted_iota(jnp.int32, (slots, map_ref.shape[1]), 0)
    hot = jnp.where(slot_ids == map_ref[...], 1.0, 0.0).astype(jnp.bfloat16)
    onehot[...] = hot
    count = jnp.dot(
        hot, jnp.ones((map_ref.shape[1], 128), jnp.bfloat16), preferred_element_type=jnp.float32
    )
    share = 1.0 / jnp.maximum(count, 1.0)

    def merge(which, store):
        sums = jnp.dot(
            onehot[...],
            tok[:, pl.ds(pl.multiple_of(which * half, 128), half)],
            preferred_element_type=jnp.float32,
        )
        for i in range(half // 128):
            cols = slice(i * 128, (i + 1) * 128)
            part = (sums[:, cols] * share).astype(jnp.bfloat16)
            store(part.reshape(SLOTS_BLK, BLK, 128), cols)

    loads[0].wait()

    def to_sib(part, cols):
        sib_tx[:, :, cols] = part

    merge(1 - core, to_sib)

    def to_own(part, cols):
        for h in range(PARTS):
            local[h][pl.ds(core * SLOTS_BLK, SLOTS_BLK), :, cols] = part[
                :, h * PART:(h + 1) * PART
            ]

    merge(core, to_own)
    onehot_t[...] = onehot[...].T
    pl.semaphore_wait(barrier, (nrow - 1) + 2 * (ncol - 1))

    def codes_copy(i, source):
        return pltpu.make_async_remote_copy(
            src_ref=codes_tx, dst_ref=codes_rx.at[source],
            send_sem=codes_ssem.at[i], recv_sem=codes_rsem.at[i],
            device_id=(lax.rem(row + ring(i), nrow), col), device_id_type=MESH,
        )

    def pair_copy(i, src, dst):
        return pltpu.make_async_remote_copy(
            src_ref=src, dst_ref=dst, send_sem=pair_ssem.at[i], recv_sem=pair_rsem.at[i],
            device_id=(sib, col), device_id_type=MESH,
        )

    code_copy = pair_copy(3, codes_tx, codes_sib)
    code_copy.start()
    sib_copy = pair_copy(0, sib_tx, sib_rx)
    sib_copy.start()

    @pl.loop(0, nrow - 1)
    def _(i):
        codes_copy(i, row).start()

    def away(t, d):
        far = 2 * (1 if fixed else slot_plan[t][0])
        return lax.rem(row + (nrow - far if d else far), nrow)

    def hop(t, d, h):
        return pltpu.make_async_remote_copy(
            src_ref=stage.at[h, d, t], dst_ref=recv.at[h, d, t],
            send_sem=hop_ssem.at[h, d, t], recv_sem=hop_rsem.at[h, d, t],
            device_id=(away(t, d), col), device_id_type=MESH,
        )

    def take(t, h):
        for d in range(2):
            hop(t, d, h).wait_recv()
            local[h][16 + 2 * t + d] = recv[h, d, t]

    def put(t, h, table=tbl_s):
        for d in range(2):
            stage[h, d, t] = local[h][table[d, t]]
            hop(t, d, h).start()

    def sib_arrived():
        sib_copy.wait_recv()
        for h in range(PARTS):
            local[h][pl.ds((1 - core) * SLOTS_BLK, SLOTS_BLK)] = sib_rx[
                :, h * PART:(h + 1) * PART
            ]

    early = 0 if fixed else sum(need == 0 for _, need in slot_plan)
    code_copy.wait_recv()
    if early:
        near = jnp.sum(codes_tx[...] + codes_sib[...], axis=0, keepdims=True)
        plan_first(near, first_v, nz)
        first_copy = pltpu.make_async_copy(first_v, first_s, load_sem.at[6])
        first_copy.start()
        sib_arrived()
        first_copy.wait()
        for t in range(early):
            for h in range(PARTS):
                put(t, h, first_s)

    nb_tx[...] = jnp.zeros((8, 128), jnp.int32)
    nb_tx[0:OWN, 0:nb_ref.shape[1]] = nb_ref[...]

    def plane_copy(i, source, src, dst, ssem, rsem):
        return pltpu.make_async_remote_copy(
            src_ref=src, dst_ref=dst.at[source], send_sem=ssem.at[i], recv_sem=rsem.at[i],
            device_id=(row, plane(i)), device_id_type=MESH,
        )

    def nb_copy(i, source):
        return plane_copy(i, source, nb_tx, nb_rx, nb_ssem, nb_rsem)

    def miss_copy(i, source):
        return plane_copy(i, source, miss_tx, miss_rx, miss_ssem, miss_rsem)

    nb_rx[col] = nb_tx[...]

    @pl.loop(0, ncol - 1)
    def _(i):
        nb_copy(i, col).start()

    @pl.loop(0, nrow - 1)
    def _(i):
        codes_copy(i, lax.rem(row + nrow - ring(i), nrow)).wait_recv()

    place = jnp.sum(jnp.sum(codes_rx[...], axis=0), axis=0, keepdims=True)
    miss_tx[...] = plan_routes(place, tbl_v, nz, z, slot_plan, fixed)
    tbl_copy = pltpu.make_async_copy(tbl_v, tbl_s, load_sem.at[4])
    tbl_copy.start()
    tbl_copy.wait()
    if not early:
        sib_arrived()
    needs = [need for _, need in slot_plan]

    def put_late(t, h):
        if fixed or t >= early:
            put(t, h)

    in_turn(needs, PARTS, FIXED_LAG if fixed else 0, put_late, take)

    for j in range(OWN):
        for h in range(PARTS):
            fin_tx[j, h * PART:(h + 1) * PART] = local[h][tbl_s[3, OWN * (1 - core) + j]]
    fin_copy = pair_copy(1, fin_tx, fin_rx)
    fin_copy.start()
    for j in range(OWN):
        for h in range(PARTS):
            base = j * BLK + h * PART
            owned[core, base:base + PART] = local[h][tbl_s[3, OWN * core + j]]
    for load in loads[1:]:
        load.wait()

    kv_rows = OWN * BLK

    def msg_copy(other, source):
        return pltpu.make_async_remote_copy(
            src_ref=msg_tx.at[other], dst_ref=msg_rx.at[source],
            send_sem=msg_ssem.at[other], recv_sem=msg_rsem.at[source],
            device_id=(row, other), device_id_type=MESH,
        )

    def keep(source):
        pairs[pl.ds(OWN * source, OWN)] = msg_rx[source, 0:kv_rows].reshape(OWN, BLK, 128)

    def product(which, i, group):
        return jnp.dot(
            owned[which],
            wts[
                i,
                pl.ds(pl.multiple_of(which * half, 128), half),
                pl.ds(pl.multiple_of(group * hw, 128), hw),
            ],
            preferred_element_type=jnp.float32,
        )

    groups = [lax.rem(col + g, 2) for g in range(2)]
    begun = [[product(core, i, group) for i in range(3)] for group in groups]
    fin_copy.wait_recv()
    for j in range(OWN):
        owned[1 - core, j * BLK:(j + 1) * BLK] = fin_rx[j]
    for group, sums in zip(groups, begun):
        query, key, value = (
            (sums[i] + product(1 - core, i, group)).astype(jnp.bfloat16) for i in range(3)
        )
        for h in range(hh):
            cols = slice(h * HD, (h + 1) * HD)
            packed = jnp.concatenate([key[:, cols], value[:, cols]], axis=1)
            for j in range(OWN):
                q = query[j * BLK:(j + 1) * BLK, cols]
                to = half_col * group + OWN * h + j
                msg_tx[to, 0:kv_rows] = packed
                msg_tx[to, kv_rows:kv_rows + BLK // 2] = jnp.concatenate(
                    [q[: BLK // 2], q[BLK // 2:]], axis=1
                )

        @pl.loop(0, half_col)
        def _(i):
            other = half_col * group + lax.rem(col + half_col // 2 + i, half_col)

            @pl.when(other != col)
            def _():
                msg_copy(other, col).start()

    msg_rx[col] = msg_tx[col]
    keep(col)

    @pl.loop(0, ncol - 1)
    def _(i):
        nb_copy(i, plane(i, -1)).wait_recv()

    nb_load = pltpu.make_async_copy(nb_rx, nb_s, load_sem.at[5])
    nb_load.start()
    nb_load.wait()

    @pl.loop(0, ncol - 1)
    def _(i):
        source = lax.rem(col + 1 + i, ncol)
        msg_copy(source, source).wait_recv()
        keep(source)

    slot_q = lax.rem(col, OWN)
    to_core = col // half_col
    here = to_core == core
    low = lax.broadcasted_iota(jnp.int32, (BLK // 2, 128), 1) < HD
    factor = math.log2(math.e) / math.sqrt(HD)
    nb_count = nb_ref.shape[1]

    def att_copy(i):
        other = plane(i)
        return pltpu.make_async_remote_copy(
            src_ref=att_tx.at[other],
            dst_ref=att_rx.at[core * half_col + lax.rem(col, half_col)],
            send_sem=att_ssem.at[i],
            recv_sem=att_rsem.at[core * half_col + lax.rem(col, half_col)],
            device_id=(2 * z + to_core, other), device_id_type=MESH,
        )

    def attend(other):
        q2 = msg_rx[other, kv_rows:kv_rows + BLK // 2].astype(jnp.float32)
        q = jnp.concatenate(
            [jnp.where(low, q2, 0.0), jnp.where(low, pltpu.roll(q2, HD, 1), 0.0)], axis=0
        ).astype(jnp.bfloat16)
        kv = jnp.concatenate([pairs[nb_s[other, slot_q, n]] for n in range(nb_count)], axis=0)
        score = lax.dot_general(
            q, kv, (((1,), (1,)), ((), ())), preferred_element_type=jnp.float32
        )
        top = jnp.max(score, axis=1, keepdims=True)
        prob = jnp.exp2((score - top) * factor)
        total = jnp.sum(prob, axis=1, keepdims=True)
        mix = jnp.dot(prob.astype(jnp.bfloat16), kv, preferred_element_type=jnp.float32) / total
        upper, lower = mix[: BLK // 2], mix[BLK // 2:]
        return jnp.where(low, pltpu.roll(upper, HD, 1), lower).astype(jnp.bfloat16)

    @pl.loop(0, ncol, step=TOGETHER)
    def _(first):
        done = [attend(plane(first + n)) for n in range(TOGETHER)]
        for n in range(TOGETHER):
            att_tx[plane(first + n)] = done[n]
        for n in range(TOGETHER):
            i = first + n

            @pl.when(jnp.logical_or(i < ncol - 1, jnp.logical_not(here)))
            def _(i=i):
                att_copy(i).start()

    @pl.when(here)
    def _():
        att_rx[core * half_col + lax.rem(col, half_col)] = att_tx[col]

    def att_wait(i):
        pltpu.make_async_remote_copy(
            src_ref=att_tx.at[0], dst_ref=att_rx.at[i],
            send_sem=att_ssem.at[0], recv_sem=att_rsem.at[i],
            device_id=(row, col), device_id_type=MESH,
        ).wait_recv()

    @pl.loop(0, ncol)
    def _(i):
        own_turn = jnp.logical_and(here, i == core * half_col + lax.rem(col, half_col))

        @pl.when(jnp.logical_not(own_turn))
        def _():
            att_wait(i)

    for k in range(2):
        for j in range(OWN):
            for p in range(hh // 2):
                a = att_rx[k * half_col + (2 * p) * OWN + j].astype(jnp.float32)
                b = att_rx[k * half_col + (2 * p + 1) * OWN + j].astype(jnp.float32)
                cols = slice(p * 128, (p + 1) * 128)
                to = 2 * steps + k * OWN + j
                home[0][to, :, cols] = jnp.where(low, a, pltpu.roll(b, HD, 1)).astype(jnp.bfloat16)
                home[1][to, :, cols] = jnp.where(low, pltpu.roll(a, HD, 1), b).astype(jnp.bfloat16)

    def ret(t, d, h):
        return pltpu.make_async_remote_copy(
            src_ref=ret_stage.at[h, d, t], dst_ref=ret_recv.at[h, d, t],
            send_sem=ret_ssem.at[h, d, t], recv_sem=ret_rsem.at[h, d, t],
            device_id=(away(t, 1 - d), col), device_id_type=MESH,
        )

    def ret_take(s, h):
        t = steps - 1 - s
        for d in range(2):
            ret(t, d, h).wait_recv()
            home[h][2 * t + d] = ret_recv[h, d, t]

    def ret_put(s, h):
        t = steps - 1 - s
        for d in range(2):
            ret_stage[h, d, t] = home[h][tbl_s[2, 16 + 2 * t + d]]
            ret(t, d, h).start()
        if not fixed and s == 1 and h == 0:
            tell()

    def tell():
        @pl.loop(0, ncol - 1)
        def _(i):
            miss_copy(i, col).start()

    if fixed:
        tell()
    ret_needs = [
        steps - min([u for u in range(steps) if needs[u] > t], default=steps)
        for t in reversed(range(steps))
    ]
    in_turn(ret_needs, 2, FIXED_LAG if fixed else 0, ret_put, ret_take)

    for b in range(SLOTS_BLK):
        at = tbl_s[2, (1 - core) * SLOTS_BLK + b]
        for h in range(2):
            ret_tx[b, h * (BLK // 2):(h + 1) * (BLK // 2)] = home[h][at]
    ret_copy = pair_copy(2, ret_tx, ret_rx)
    ret_copy.start()
    mine = jnp.concatenate(
        [home[h][tbl_s[2, core * SLOTS_BLK + b]] for b in range(SLOTS_BLK) for h in range(2)], axis=0
    )
    hot_t = onehot_t[...]
    out_ref[:, pl.ds(pl.multiple_of(core * hw, 128), hw)] = jnp.dot(
        hot_t, mine, preferred_element_type=jnp.float32
    ).astype(jnp.bfloat16)
    miss_rx[col] = miss_tx[...]

    @pl.loop(0, ncol - 1)
    def _(i):
        miss_copy(i, plane(i, -1)).wait_recv()

    first_v[...] = jnp.max(miss_rx[...], axis=0)
    miss_load = pltpu.make_async_copy(first_v, miss_s, load_sem.at[7])
    miss_load.start()
    miss_load.wait()
    flag_ref[0] = miss_s[0, 0]
    ret_copy.wait_recv()
    out_ref[:, pl.ds(pl.multiple_of((1 - core) * hw, 128), hw)] = jnp.dot(
        hot_t, ret_rx[...].reshape(slots, hw), preferred_element_type=jnp.float32
    ).astype(jnp.bfloat16)

    code_copy.wait_send()
    sib_copy.wait_send()
    fin_copy.wait_send()
    ret_copy.wait_send()

    @pl.loop(0, nrow - 1)
    def _(i):
        codes_copy(i, row).wait_send()

    @pl.loop(0, ncol - 1)
    def _(i):
        nb_copy(i, col).wait_send()
        miss_copy(i, col).wait_send()
        msg_copy(lax.rem(col + 1 + i, ncol), col).wait_send()

    @pl.loop(0, ncol)
    def _(i):
        @pl.when(jnp.logical_or(i < ncol - 1, jnp.logical_not(here)))
        def _():
            att_copy(i).wait_send()

    def sent(t):
        for d in range(2):
            for h in range(PARTS):
                hop(t, d, h).wait_send()
            for h in range(2):
                ret(t, d, h).wait_send()

    if fixed:
        pl.loop(0, steps)(sent)
    else:
        for t in range(steps):
            sent(t)


def routed(fixed, tokens, merge_map, block_owner, neighbours, w_query, w_key, w_value):
    nrow, ncol = lax.axis_size("row"), lax.axis_size("col")
    count, width = tokens.shape
    head_width = w_query.shape[1]
    heads = head_width // HD
    half, hw = width // 2, head_width // 2
    bf, i32 = jnp.bfloat16, jnp.int32
    if fixed:
        slot_plan = tuple((1, max(0, t - FIXED_LAG + 1)) for t in range(nrow))
    else:
        slot_plan = tuple(zip(DIST, NEED))
    steps = len(slot_plan)
    places = 16 + 2 * steps
    hbm = pl.BlockSpec(memory_space=pl.ANY)
    vmem = pl.BlockSpec(memory_space=pltpu.VMEM)
    smem = pl.BlockSpec(memory_space=pltpu.SMEM)
    dma = pltpu.SemaphoreType.DMA
    msg_rows = OWN * BLK + BLK // 2
    slots = SLOTS_BLK * BLK
    scratch = [
        pltpu.VMEM((count, width), bf),
        pltpu.VMEM((3, width, head_width), bf),
        pltpu.VMEM((1, count), i32),
        pltpu.SMEM(block_owner.shape, i32),
        pltpu.VMEM(neighbours.shape, i32),
        pltpu.VMEM((slots, count), bf),
        pltpu.VMEM((count, slots), bf),
        pltpu.VMEM((8, 128), i32),
        pltpu.VMEM((nrow, 8, 128), i32),
        pltpu.VMEM((8, 128), i32),
        pltpu.VMEM((8, 128), i32),
        pltpu.SMEM((8, 128), i32),
        pltpu.VMEM((8, 128), i32),
        pltpu.SMEM((8, 128), i32),
        pltpu.VMEM((SLOTS_BLK, BLK, half), bf),
        pltpu.VMEM((SLOTS_BLK, BLK, half), bf),
        pltpu.VMEM((PARTS, 2, steps, PART, half), bf),
        pltpu.VMEM((PARTS, 2, steps, PART, half), bf),
        pltpu.VMEM((OWN, BLK, half), bf),
        pltpu.VMEM((OWN, BLK, half), bf),
        pltpu.VMEM((2, OWN * BLK, half), bf),
        pltpu.VMEM((ncol, msg_rows, 128), bf),
        pltpu.VMEM((ncol, msg_rows, 128), bf),
        pltpu.VMEM((OWN * ncol, BLK, 128), bf),
        pltpu.VMEM((8, 128), i32),
        pltpu.VMEM((ncol, 8, 128), i32),
        pltpu.SMEM((ncol, 8, 128), i32),
        pltpu.VMEM((8, 128), i32),
        pltpu.VMEM((ncol, 8, 128), i32),
        pltpu.SMEM((8, 128), i32),
        pltpu.VMEM((ncol, BLK // 2, 128), bf),
        pltpu.VMEM((ncol, BLK // 2, 128), bf),
        pltpu.VMEM((2, 2, steps, BLK // 2, hw), bf),
        pltpu.VMEM((2, 2, steps, BLK // 2, hw), bf),
        pltpu.VMEM((SLOTS_BLK, BLK, hw), bf),
        pltpu.VMEM((SLOTS_BLK, BLK, hw), bf),
        dma((11,)),
        dma((nrow,)), dma((nrow,)),
        dma((4,)), dma((4,)),
        dma((PARTS, 2, steps)), dma((PARTS, 2, steps)),
        dma((ncol,)), dma((ncol,)),
        dma((ncol,)), dma((ncol,)),
        dma((ncol,)), dma((ncol,)),
        dma((ncol + 1,)), dma((ncol,)),
        dma((2, 2, steps)), dma((2, 2, steps)),
        *[pltpu.VMEM((places, PART, half), bf)] * PARTS,
        *[pltpu.VMEM((2 * steps + 2 * OWN, BLK // 2, hw), bf)] * 2,
    ]
    return pl.pallas_call(
        functools.partial(kernel, (nrow, ncol, heads, width, slot_plan, fixed)),
        out_shape=(
            jax.ShapeDtypeStruct((count, head_width), bf),
            jax.ShapeDtypeStruct((1,), i32),
        ),
        in_specs=[hbm] * 7,
        out_specs=(vmem, smem),
        scratch_shapes=scratch,
        compiler_params=pltpu.CompilerParams(
            collective_id=int(fixed), has_side_effects=True, vmem_limit_bytes=56 * 1024 * 1024
        ),
    )(tokens, merge_map.reshape(1, count), block_owner, neighbours, w_query, w_key, w_value)


def program(*args):
    out, missed = routed(False, *args)
    return lax.cond(missed[0] > 0, lambda: routed(True, *args)[0], lambda: out)


def solution(mesh):
    in_specs = (
        P(("row", "col"), None),
        P(("row", "col")),
        P(("row", "col"), None),
        P(("row", "col"), None),
        P(),
        P(),
        P(),
    )
    out_specs = P(("row", "col"), None)
    return jax.shard_map(
        program, mesh=mesh, in_specs=in_specs, out_specs=out_specs, check_vma=False
    )
```

```python
import functools
import math

import jax
import jax.numpy as jnp
from jax import lax
from jax.experimental import pallas as pl
from jax.experimental.pallas import tpu as pltpu
from jax.sharding import PartitionSpec as P

HD = 64
BLK = 64
OWN = 2
SLOTS_BLK = 8
PARTS = 2
PART = BLK // PARTS
TOGETHER = 4
MESH = pl.DeviceIdType.MESH
DIST = (1, 2, 1, 1, 2, 1, 1, 2, 1, 1, 1, 2, 2, 1, 1, 1)
NEED = (0, 0, 0, 0, 1, 2, 3, 5, 7, 7, 8, 9, 11, 12, 13, 14)
FIXED_LAG = 3


def plan_start(place, nz, rows):
    shape = (rows, 128)
    place = jnp.broadcast_to(place, shape)
    lane = lax.broadcasted_iota(jnp.int32, shape, 1)
    valid = place > 0
    place = jnp.where(valid, place - 1, 0)
    pos = place >> 4
    fwd = ((lane >> 2) - pos) & (nz - 1)
    half = nz // 2
    right = (fwd < half) | ((fwd == half) & ((lane & 1) == 0))
    rem = jnp.where(valid, jnp.where(right, fwd, nz - fwd), 0)
    return lane, pos, jnp.where(right, 0, 1), rem, place & 15


def plan_first(place, tbl_v, nz):
    lane, _, way, rem, loc = plan_start(place, nz, 8)
    row = lax.broadcasted_iota(jnp.int32, (8, 128), 0)
    send = jnp.zeros((8, 128), jnp.int32)
    left = jnp.where(way == row, rem, 0)
    for t in range(len(DIST)):
        if NEED[t] == 0:
            key = jnp.where(left >= DIST[t], left * 128 + lane + 1, 0)
            best = jnp.max(key, axis=1, keepdims=True)
            pick = (key == best) & (key > 0)
            own = jnp.sum(jnp.where(pick, loc, 0), axis=1, keepdims=True)
            send = jnp.where(lane == t, own, send)
            left = jnp.where(pick, 0, left)
    tbl_v[...] = send


def plan_routes(place, tbl_v, nz, z, slots, fixed):
    rows = max(2 * nz, 8)
    shape = (rows, 128)
    lane, pos, way, rem, loc = plan_start(place, nz, rows)
    row = lax.broadcasted_iota(jnp.int32, shape, 0)
    row_way = jnp.where(row >= nz, 1, 0)
    at = pos + nz * way
    sign = 1 - 2 * way
    ready = jnp.zeros(shape, jnp.int32)
    send = jnp.zeros(shape, jnp.int32)
    back = jnp.full(shape, -1, jnp.int32)
    for t, (dist, need) in enumerate(slots):
        go = (at == row) & (rem >= dist) & (ready <= need)
        if fixed:
            go = go & (rem == nz // 2 - t // 4) & ((lane & 3) == t % 4)
        key = jnp.where(go, rem * 128 + lane + 1, 0)
        best = jnp.max(key, axis=1, keepdims=True)
        pick = jnp.where(key == best, jnp.minimum(key, 1), 0)
        moved = jnp.broadcast_to(jnp.max(pick, axis=0, keepdims=True), shape) > 0
        own = jnp.broadcast_to(jnp.sum(pick * (loc + 1), axis=1, keepdims=True), shape)
        send = jnp.where(lane == t, own, send)
        back = jnp.where(lane == own - 1, 2 * t + row_way, back)
        at = jnp.where(moved, (at & nz) | ((at + dist * sign) & (nz - 1)), at)
        rem = jnp.where(moved, rem - dist, rem)
        ready = jnp.where(moved, t + 1, ready)
        loc = jnp.where(moved, 16 + 2 * t + way, loc)
    count = len(slots)

    def line(value):
        return jnp.broadcast_to(value, (8, 128))

    right = line(jnp.sum(jnp.where(row == z, send, 0), axis=0, keepdims=True))
    left = line(jnp.sum(jnp.where(row == z + nz, send, 0), axis=0, keepdims=True))
    here = (row == z) | (row == z + nz)
    home = line(jnp.max(jnp.where(here, back, -1), axis=0, keepdims=True))
    home = jnp.where(home < 0, 2 * count, home)
    lane8 = lane[:8]
    final = jnp.zeros((8, 128), jnp.int32)
    for i in range(2 * OWN):
        end = jnp.sum(jnp.where(lane == 2 * OWN * z + i, loc, 0), axis=1, keepdims=True)[:8]
        home = jnp.where(lane8 == end, 2 * count + i, home)
        final = jnp.where(lane8 == i, end, final)
    row8 = row[:8]
    table = jnp.where(row8 == 0, jnp.maximum(right - 1, 0), jnp.maximum(left - 1, 0))
    tbl_v[...] = jnp.where(row8 < 2, table, jnp.where(row8 == 2, home, final))
    return line(jnp.max(rem, axis=1, keepdims=True)[:8])


def in_turn(slots, parts, lag, put, take):
    count = len(slots)
    if lag:
        for t in range(lag):
            for h in range(parts):
                put(t, h)

        @pl.loop(lag, count)
        def _(t):
            for h in range(parts):
                take(t - lag, h)
                put(t, h)

        for t in range(count - lag, count):
            for h in range(parts):
                take(t, h)
        return
    done = 0
    for t, need in enumerate(slots):
        for h in range(parts):
            for u in range(done, need):
                take(u, h)
            put(t, h)
        done = max(done, need)
    for u in range(done, count):
        for h in range(parts):
            take(u, h)


def kernel(
    dims,
    tokens_hbm, map_hbm, owner_hbm, nb_hbm, wq_hbm, wk_hbm, wv_hbm,
    out_ref, flag_ref,
    tok, wts, map_ref, owner_ref, nb_ref, onehot, onehot_t,
    codes_tx, codes_rx, codes_sib, tbl_v, tbl_s, first_v, first_s,
    sib_tx, sib_rx, stage, recv, fin_tx, fin_rx, owned,
    msg_tx, msg_rx, pairs, nb_tx, nb_rx, nb_s, miss_tx, miss_rx, miss_s,
    att_tx, att_rx, ret_stage, ret_recv, ret_tx, ret_rx,
    load_sem, codes_ssem, codes_rsem, pair_ssem, pair_rsem, hop_ssem, hop_rsem,
    msg_ssem, msg_rsem, nb_ssem, nb_rsem, miss_ssem, miss_rsem, att_ssem, att_rsem,
    ret_ssem, ret_rsem, *kept,
):
    nrow, ncol, heads, width, slot_plan, fixed = dims
    nz = nrow // 2
    steps = len(slot_plan)
    local, home = kept[:PARTS], kept[PARTS:]
    side = math.isqrt(ncol)
    half = width // 2
    hh = heads // 2
    hw = hh * HD
    half_col = ncol // 2
    slots = SLOTS_BLK * BLK
    row = lax.axis_index("row")
    col = lax.axis_index("col")
    z = row // 2
    core = lax.rem(row, 2)
    sib = row + 1 - 2 * core
    barrier = pltpu.get_barrier_semaphore()

    small = [
        pltpu.make_async_copy(src, dst, load_sem.at[8 + i])
        for i, (src, dst) in enumerate(
            ((owner_hbm, owner_ref), (map_hbm, map_ref), (nb_hbm, nb_ref))
        )
    ]
    for copy in small:
        copy.start()
    loads = [pltpu.make_async_copy(tokens_hbm, tok, load_sem.at[0])]
    for i, w in enumerate((wq_hbm, wk_hbm, wv_hbm)):
        loads.append(pltpu.make_async_copy(w, wts.at[i], load_sem.at[i + 1]))
    for load in loads:
        load.start()

    def ring(i):
        return nrow // 2 + ((i + 1) // 2) * (1 - 2 * lax.rem(i, 2))

    def plane(i, sign=1):
        dx, dy = (0x36 >> (2 * (i // side))) & 3, (0x36 >> (2 * lax.rem(i, side))) & 3
        x = lax.rem(col // side + side + sign * dx, side)
        y = lax.rem(lax.rem(col, side) + side + sign * dy, side)
        return x * side + y

    @pl.loop(0, nrow - 1)
    def _(i):
        pl.semaphore_signal(
            barrier, inc=1, device_id=(lax.rem(row + ring(i), nrow), col), device_id_type=MESH
        )

    @pl.loop(0, ncol - 1)
    def _(i):
        other = plane(i)
        pl.semaphore_signal(barrier, inc=1, device_id=(row, other), device_id_type=MESH)
        pl.semaphore_signal(barrier, inc=1, device_id=(sib, other), device_id_type=MESH)

    for copy in small:
        copy.wait()

    lane8 = lax.broadcasted_iota(jnp.int32, (8, 128), 1)
    row8 = lax.broadcasted_iota(jnp.int32, (8, 128), 0)
    codes = jnp.zeros((8, 128), jnp.int32)
    for b in range(SLOTS_BLK):
        codes = jnp.where((lane8 == owner_ref[0, b]) & (row8 == 0), row * 8 + b + 1, codes)
    codes_tx[...] = codes
    codes_rx[row] = codes

    slot_ids = lax.broadcasted_iota(jnp.int32, (slots, map_ref.shape[1]), 0)
    hot = jnp.where(slot_ids == map_ref[...], 1.0, 0.0).astype(jnp.bfloat16)
    onehot[...] = hot
    count = jnp.dot(
        hot, jnp.ones((map_ref.shape[1], 128), jnp.bfloat16), preferred_element_type=jnp.float32
    )
    share = 1.0 / jnp.maximum(count, 1.0)

    def merge(which, store):
        sums = jnp.dot(
            onehot[...],
            tok[:, pl.ds(pl.multiple_of(which * half, 128), half)],
            preferred_element_type=jnp.float32,
        )
        for i in range(half // 128):
            cols = slice(i * 128, (i + 1) * 128)
            part = (sums[:, cols] * share).astype(jnp.bfloat16)
            store(part.reshape(SLOTS_BLK, BLK, 128), cols)

    loads[0].wait()

    def to_sib(part, cols):
        sib_tx[:, :, cols] = part

    merge(1 - core, to_sib)

    def to_own(part, cols):
        for h in range(PARTS):
            local[h][pl.ds(core * SLOTS_BLK, SLOTS_BLK), :, cols] = part[
                :, h * PART:(h + 1) * PART
            ]

    merge(core, to_own)
    onehot_t[...] = onehot[...].T
    pl.semaphore_wait(barrier, (nrow - 1) + 2 * (ncol - 1))

    def codes_copy(i, source):
        return pltpu.make_async_remote_copy(
            src_ref=codes_tx, dst_ref=codes_rx.at[source],
            send_sem=codes_ssem.at[i], recv_sem=codes_rsem.at[i],
            device_id=(lax.rem(row + ring(i), nrow), col), device_id_type=MESH,
        )

    def pair_copy(i, src, dst):
        return pltpu.make_async_remote_copy(
            src_ref=src, dst_ref=dst, send_sem=pair_ssem.at[i], recv_sem=pair_rsem.at[i],
            device_id=(sib, col), device_id_type=MESH,
        )

    code_copy = pair_copy(3, codes_tx, codes_sib)
    code_copy.start()
    sib_copy = pair_copy(0, sib_tx, sib_rx)
    sib_copy.start()

    @pl.loop(0, nrow - 1)
    def _(i):
        codes_copy(i, row).start()

    def away(t, d):
        far = 2 * (1 if fixed else slot_plan[t][0])
        return lax.rem(row + (nrow - far if d else far), nrow)

    def hop(t, d, h):
        return pltpu.make_async_remote_copy(
            src_ref=stage.at[h, d, t], dst_ref=recv.at[h, d, t],
            send_sem=hop_ssem.at[h, d, t], recv_sem=hop_rsem.at[h, d, t],
            device_id=(away(t, d), col), device_id_type=MESH,
        )

    def take(t, h):
        for d in range(2):
            hop(t, d, h).wait_recv()
            local[h][16 + 2 * t + d] = recv[h, d, t]

    def put(t, h, table=tbl_s):
        for d in range(2):
            stage[h, d, t] = local[h][table[d, t]]
            hop(t, d, h).start()

    def sib_arrived():
        sib_copy.wait_recv()
        for h in range(PARTS):
            local[h][pl.ds((1 - core) * SLOTS_BLK, SLOTS_BLK)] = sib_rx[
                :, h * PART:(h + 1) * PART
            ]

    early = 0 if fixed else sum(need == 0 for _, need in slot_plan)
    code_copy.wait_recv()
    if early:
        near = jnp.sum(codes_tx[...] + codes_sib[...], axis=0, keepdims=True)
        plan_first(near, first_v, nz)
        first_copy = pltpu.make_async_copy(first_v, first_s, load_sem.at[6])
        first_copy.start()
        sib_arrived()
        first_copy.wait()
        for t in range(early):
            for h in range(PARTS):
                put(t, h, first_s)

    nb_tx[...] = jnp.zeros((8, 128), jnp.int32)
    nb_tx[0:OWN, 0:nb_ref.shape[1]] = nb_ref[...]

    def plane_copy(i, source, src, dst, ssem, rsem):
        return pltpu.make_async_remote_copy(
            src_ref=src, dst_ref=dst.at[source], send_sem=ssem.at[i], recv_sem=rsem.at[i],
            device_id=(row, plane(i)), device_id_type=MESH,
        )

    def nb_copy(i, source):
        return plane_copy(i, source, nb_tx, nb_rx, nb_ssem, nb_rsem)

    def miss_copy(i, source):
        return plane_copy(i, source, miss_tx, miss_rx, miss_ssem, miss_rsem)

    nb_rx[col] = nb_tx[...]

    @pl.loop(0, ncol - 1)
    def _(i):
        nb_copy(i, col).start()

    @pl.loop(0, nrow - 1)
    def _(i):
        codes_copy(i, lax.rem(row + nrow - ring(i), nrow)).wait_recv()

    place = jnp.sum(jnp.sum(codes_rx[...], axis=0), axis=0, keepdims=True)
    miss_tx[...] = plan_routes(place, tbl_v, nz, z, slot_plan, fixed)
    tbl_copy = pltpu.make_async_copy(tbl_v, tbl_s, load_sem.at[4])
    tbl_copy.start()
    tbl_copy.wait()
    if not early:
        sib_arrived()
    needs = [need for _, need in slot_plan]

    def put_late(t, h):
        if fixed or t >= early:
            put(t, h)

    in_turn(needs, PARTS, FIXED_LAG if fixed else 0, put_late, take)

    for j in range(OWN):
        for h in range(PARTS):
            fin_tx[j, h * PART:(h + 1) * PART] = local[h][tbl_s[3, OWN * (1 - core) + j]]
    fin_copy = pair_copy(1, fin_tx, fin_rx)
    fin_copy.start()
    for j in range(OWN):
        for h in range(PARTS):
            base = j * BLK + h * PART
            owned[core, base:base + PART] = local[h][tbl_s[3, OWN * core + j]]
    for load in loads[1:]:
        load.wait()

    kv_rows = OWN * BLK

    def msg_copy(other, source):
        return pltpu.make_async_remote_copy(
            src_ref=msg_tx.at[other], dst_ref=msg_rx.at[source],
            send_sem=msg_ssem.at[other], recv_sem=msg_rsem.at[source],
            device_id=(row, other), device_id_type=MESH,
        )

    def keep(source):
        pairs[pl.ds(OWN * source, OWN)] = msg_rx[source, 0:kv_rows].reshape(OWN, BLK, 128)

    def product(which, i, group):
        return jnp.dot(
            owned[which],
            wts[
                i,
                pl.ds(pl.multiple_of(which * half, 128), half),
                pl.ds(pl.multiple_of(group * hw, 128), hw),
            ],
            preferred_element_type=jnp.float32,
        )

    groups = [lax.rem(col + g, 2) for g in range(2)]
    begun = [[product(core, i, group) for i in range(3)] for group in groups]
    fin_copy.wait_recv()
    for j in range(OWN):
        owned[1 - core, j * BLK:(j + 1) * BLK] = fin_rx[j]
    for group, sums in zip(groups, begun):
        query, key, value = (
            (sums[i] + product(1 - core, i, group)).astype(jnp.bfloat16) for i in range(3)
        )
        for h in range(hh):
            cols = slice(h * HD, (h + 1) * HD)
            packed = jnp.concatenate([key[:, cols], value[:, cols]], axis=1)
            for j in range(OWN):
                q = query[j * BLK:(j + 1) * BLK, cols]
                to = half_col * group + OWN * h + j
                msg_tx[to, 0:kv_rows] = packed
                msg_tx[to, kv_rows:kv_rows + BLK // 2] = jnp.concatenate(
                    [q[: BLK // 2], q[BLK // 2:]], axis=1
                )

        @pl.loop(0, half_col)
        def _(i):
            other = half_col * group + lax.rem(col + half_col // 2 + i, half_col)

            @pl.when(other != col)
            def _():
                msg_copy(other, col).start()

    msg_rx[col] = msg_tx[col]
    keep(col)

    @pl.loop(0, ncol - 1)
    def _(i):
        nb_copy(i, plane(i, -1)).wait_recv()

    nb_load = pltpu.make_async_copy(nb_rx, nb_s, load_sem.at[5])
    nb_load.start()
    nb_load.wait()

    @pl.loop(0, ncol - 1)
    def _(i):
        source = lax.rem(col + 1 + i, ncol)
        msg_copy(source, source).wait_recv()
        keep(source)

    slot_q = lax.rem(col, OWN)
    to_core = col // half_col
    here = to_core == core
    low = lax.broadcasted_iota(jnp.int32, (BLK // 2, 128), 1) < HD
    factor = math.log2(math.e) / math.sqrt(HD)
    nb_count = nb_ref.shape[1]

    def att_copy(i):
        other = plane(i)
        return pltpu.make_async_remote_copy(
            src_ref=att_tx.at[other],
            dst_ref=att_rx.at[core * half_col + lax.rem(col, half_col)],
            send_sem=att_ssem.at[i],
            recv_sem=att_rsem.at[core * half_col + lax.rem(col, half_col)],
            device_id=(2 * z + to_core, other), device_id_type=MESH,
        )

    def attend(other):
        q2 = msg_rx[other, kv_rows:kv_rows + BLK // 2].astype(jnp.float32)
        q = jnp.concatenate(
            [jnp.where(low, q2, 0.0), jnp.where(low, pltpu.roll(q2, HD, 1), 0.0)], axis=0
        ).astype(jnp.bfloat16)
        kv = jnp.concatenate([pairs[nb_s[other, slot_q, n]] for n in range(nb_count)], axis=0)
        score = lax.dot_general(
            q, kv, (((1,), (1,)), ((), ())), preferred_element_type=jnp.float32
        )
        top = jnp.max(score, axis=1, keepdims=True)
        prob = jnp.exp2((score - top) * factor)
        total = jnp.sum(prob, axis=1, keepdims=True)
        mix = jnp.dot(prob.astype(jnp.bfloat16), kv, preferred_element_type=jnp.float32) / total
        upper, lower = mix[: BLK // 2], mix[BLK // 2:]
        return jnp.where(low, pltpu.roll(upper, HD, 1), lower).astype(jnp.bfloat16)

    @pl.loop(0, ncol, step=TOGETHER)
    def _(first):
        done = [attend(plane(first + n)) for n in range(TOGETHER)]
        for n in range(TOGETHER):
            att_tx[plane(first + n)] = done[n]
        for n in range(TOGETHER):
            i = first + n

            @pl.when(jnp.logical_or(i < ncol - 1, jnp.logical_not(here)))
            def _(i=i):
                att_copy(i).start()

    @pl.when(here)
    def _():
        att_rx[core * half_col + lax.rem(col, half_col)] = att_tx[col]

    def att_wait(i):
        pltpu.make_async_remote_copy(
            src_ref=att_tx.at[0], dst_ref=att_rx.at[i],
            send_sem=att_ssem.at[0], recv_sem=att_rsem.at[i],
            device_id=(row, col), device_id_type=MESH,
        ).wait_recv()

    @pl.loop(0, ncol)
    def _(i):
        own_turn = jnp.logical_and(here, i == core * half_col + lax.rem(col, half_col))

        @pl.when(jnp.logical_not(own_turn))
        def _():
            att_wait(i)

    for k in range(2):
        for j in range(OWN):
            for p in range(hh // 2):
                a = att_rx[k * half_col + (2 * p) * OWN + j].astype(jnp.float32)
                b = att_rx[k * half_col + (2 * p + 1) * OWN + j].astype(jnp.float32)
                cols = slice(p * 128, (p + 1) * 128)
                to = 2 * steps + k * OWN + j
                home[0][to, :, cols] = jnp.where(low, a, pltpu.roll(b, HD, 1)).astype(jnp.bfloat16)
                home[1][to, :, cols] = jnp.where(low, pltpu.roll(a, HD, 1), b).astype(jnp.bfloat16)

    def ret(t, d, h):
        return pltpu.make_async_remote_copy(
            src_ref=ret_stage.at[h, d, t], dst_ref=ret_recv.at[h, d, t],
            send_sem=ret_ssem.at[h, d, t], recv_sem=ret_rsem.at[h, d, t],
            device_id=(away(t, 1 - d), col), device_id_type=MESH,
        )

    def ret_take(s, h):
        t = steps - 1 - s
        for d in range(2):
            ret(t, d, h).wait_recv()
            home[h][2 * t + d] = ret_recv[h, d, t]

    def ret_put(s, h):
        t = steps - 1 - s
        for d in range(2):
            ret_stage[h, d, t] = home[h][tbl_s[2, 16 + 2 * t + d]]
            ret(t, d, h).start()
        if not fixed and h == 0:
            if s == 1:
                tell()
            if s == 2:
                settle()
            if s == steps - 2:
                for u in range(steps // 2, steps):
                    for d in range(2):
                        for g in range(2):
                            ret(u, d, g).wait_send()

    def tell():
        @pl.loop(0, ncol - 1)
        def _(i):
            miss_copy(i, col).start()

    def settle():
        code_copy.wait_send()
        sib_copy.wait_send()
        fin_copy.wait_send()

        @pl.loop(0, nrow - 1)
        def _(i):
            codes_copy(i, row).wait_send()

        @pl.loop(0, ncol - 1)
        def _(i):
            nb_copy(i, col).wait_send()
            msg_copy(lax.rem(col + 1 + i, ncol), col).wait_send()

        @pl.loop(0, ncol)
        def _(i):
            @pl.when(jnp.logical_or(i < ncol - 1, jnp.logical_not(here)))
            def _():
                att_copy(i).wait_send()

        def sent(t):
            for d in range(2):
                for h in range(PARTS):
                    hop(t, d, h).wait_send()

        if fixed:
            pl.loop(0, steps)(sent)
        else:
            for t in range(steps):
                sent(t)

    if fixed:
        tell()
        settle()
    ret_needs = [
        steps - min([u for u in range(steps) if needs[u] > t], default=steps)
        for t in reversed(range(steps))
    ]
    in_turn(ret_needs, 2, FIXED_LAG if fixed else 0, ret_put, ret_take)

    for b in range(SLOTS_BLK):
        at = tbl_s[2, (1 - core) * SLOTS_BLK + b]
        for h in range(2):
            ret_tx[b, h * (BLK // 2):(h + 1) * (BLK // 2)] = home[h][at]
    ret_copy = pair_copy(2, ret_tx, ret_rx)
    ret_copy.start()
    mine = jnp.concatenate(
        [home[h][tbl_s[2, core * SLOTS_BLK + b]] for b in range(SLOTS_BLK) for h in range(2)], axis=0
    )
    hot_t = onehot_t[...]
    out_ref[:, pl.ds(pl.multiple_of(core * hw, 128), hw)] = jnp.dot(
        hot_t, mine, preferred_element_type=jnp.float32
    ).astype(jnp.bfloat16)
    miss_rx[col] = miss_tx[...]

    @pl.loop(0, ncol - 1)
    def _(i):
        miss_copy(i, plane(i, -1)).wait_recv()

    first_v[...] = jnp.max(miss_rx[...], axis=0)
    miss_load = pltpu.make_async_copy(first_v, miss_s, load_sem.at[7])
    miss_load.start()
    miss_load.wait()
    flag_ref[0] = miss_s[0, 0]
    ret_copy.wait_recv()
    out_ref[:, pl.ds(pl.multiple_of((1 - core) * hw, 128), hw)] = jnp.dot(
        hot_t, ret_rx[...].reshape(slots, hw), preferred_element_type=jnp.float32
    ).astype(jnp.bfloat16)

    ret_copy.wait_send()

    @pl.loop(0, ncol - 1)
    def _(i):
        miss_copy(i, col).wait_send()

    def returned(t):
        for d in range(2):
            for h in range(2):
                ret(t, d, h).wait_send()

    if fixed:
        pl.loop(0, steps)(returned)
    else:
        for t in range(steps // 2):
            returned(t)


def routed(fixed, tokens, merge_map, block_owner, neighbours, w_query, w_key, w_value):
    nrow, ncol = lax.axis_size("row"), lax.axis_size("col")
    count, width = tokens.shape
    head_width = w_query.shape[1]
    heads = head_width // HD
    half, hw = width // 2, head_width // 2
    bf, i32 = jnp.bfloat16, jnp.int32
    if fixed:
        slot_plan = tuple((1, max(0, t - FIXED_LAG + 1)) for t in range(nrow))
    else:
        slot_plan = tuple(zip(DIST, NEED))
    steps = len(slot_plan)
    places = 16 + 2 * steps
    hbm = pl.BlockSpec(memory_space=pl.ANY)
    vmem = pl.BlockSpec(memory_space=pltpu.VMEM)
    smem = pl.BlockSpec(memory_space=pltpu.SMEM)
    dma = pltpu.SemaphoreType.DMA
    msg_rows = OWN * BLK + BLK // 2
    slots = SLOTS_BLK * BLK
    scratch = [
        pltpu.VMEM((count, width), bf),
        pltpu.VMEM((3, width, head_width), bf),
        pltpu.VMEM((1, count), i32),
        pltpu.SMEM(block_owner.shape, i32),
        pltpu.VMEM(neighbours.shape, i32),
        pltpu.VMEM((slots, count), bf),
        pltpu.VMEM((count, slots), bf),
        pltpu.VMEM((8, 128), i32),
        pltpu.VMEM((nrow, 8, 128), i32),
        pltpu.VMEM((8, 128), i32),
        pltpu.VMEM((8, 128), i32),
        pltpu.SMEM((8, 128), i32),
        pltpu.VMEM((8, 128), i32),
        pltpu.SMEM((8, 128), i32),
        pltpu.VMEM((SLOTS_BLK, BLK, half), bf),
        pltpu.VMEM((SLOTS_BLK, BLK, half), bf),
        pltpu.VMEM((PARTS, 2, steps, PART, half), bf),
        pltpu.VMEM((PARTS, 2, steps, PART, half), bf),
        pltpu.VMEM((OWN, BLK, half), bf),
        pltpu.VMEM((OWN, BLK, half), bf),
        pltpu.VMEM((2, OWN * BLK, half), bf),
        pltpu.VMEM((ncol, msg_rows, 128), bf),
        pltpu.VMEM((ncol, msg_rows, 128), bf),
        pltpu.VMEM((OWN * ncol, BLK, 128), bf),
        pltpu.VMEM((8, 128), i32),
        pltpu.VMEM((ncol, 8, 128), i32),
        pltpu.SMEM((ncol, 8, 128), i32),
        pltpu.VMEM((8, 128), i32),
        pltpu.VMEM((ncol, 8, 128), i32),
        pltpu.SMEM((8, 128), i32),
        pltpu.VMEM((ncol, BLK // 2, 128), bf),
        pltpu.VMEM((ncol, BLK // 2, 128), bf),
        pltpu.VMEM((2, 2, steps, BLK // 2, hw), bf),
        pltpu.VMEM((2, 2, steps, BLK // 2, hw), bf),
        pltpu.VMEM((SLOTS_BLK, BLK, hw), bf),
        pltpu.VMEM((SLOTS_BLK, BLK, hw), bf),
        dma((11,)),
        dma((nrow,)), dma((nrow,)),
        dma((4,)), dma((4,)),
        dma((PARTS, 2, steps)), dma((PARTS, 2, steps)),
        dma((ncol,)), dma((ncol,)),
        dma((ncol,)), dma((ncol,)),
        dma((ncol,)), dma((ncol,)),
        dma((ncol + 1,)), dma((ncol,)),
        dma((2, 2, steps)), dma((2, 2, steps)),
        *[pltpu.VMEM((places, PART, half), bf)] * PARTS,
        *[pltpu.VMEM((2 * steps + 2 * OWN, BLK // 2, hw), bf)] * 2,
    ]
    return pl.pallas_call(
        functools.partial(kernel, (nrow, ncol, heads, width, slot_plan, fixed)),
        out_shape=(
            jax.ShapeDtypeStruct((count, head_width), bf),
            jax.ShapeDtypeStruct((1,), i32),
        ),
        in_specs=[hbm] * 7,
        out_specs=(vmem, smem),
        scratch_shapes=scratch,
        compiler_params=pltpu.CompilerParams(
            collective_id=int(fixed), has_side_effects=True, vmem_limit_bytes=56 * 1024 * 1024
        ),
    )(tokens, merge_map.reshape(1, count), block_owner, neighbours, w_query, w_key, w_value)


def program(*args):
    out, missed = routed(False, *args)
    return lax.cond(missed[0] > 0, lambda: routed(True, *args)[0], lambda: out)


def solution(mesh):
    in_specs = (
        P(("row", "col"), None),
        P(("row", "col")),
        P(("row", "col"), None),
        P(("row", "col"), None),
        P(),
        P(),
        P(),
    )
    out_specs = P(("row", "col"), None)
    return jax.shard_map(
        program, mesh=mesh, in_specs=in_specs, out_specs=out_specs, check_vma=False
    )
```
